128 devices in a mesh: seq: 4 (over x), col: 32 (over z, y, core).
Axes of the slice: x: 4, y: 4, z: 4, core: 2. Of those that a mesh axis runs over, the one named last changes fastest.
Arguments:
- byte_in: bfloat16 [4, 4096, 1536], P('seq', 'col'), may hold values from -6 to 6
- flags: int32 [4, 4096], P('seq', 'col'), may hold values from 0 to 1, as said below
- fine_gain: float32 [1536], replicated, may hold values from 0.5 to 1.5
- fine_qkv: bfloat16 [1536, 3, 1536], replicated, may hold values from -1.6329932 to 1.6329932
- fine_out: bfloat16 [1536, 1536], replicated, may hold values from -0.15625 to 0.15625
- up_weight: bfloat16 [1536, 8192], P('seq', 'col'), may hold values from -0.15625 to 0.15625
- coarse_gain: float32 [8192], replicated, may hold values from 0.5 to 1.5
- q_weight: bfloat16 [8192, 8192], P('seq', 'col'), may hold values from -0.70710678 to 0.70710678
- kv_weight: bfloat16 [8192, 2, 1024], P('seq', None, 'col'), may hold values from -0.055242717 to 0.055242717
- out_weight: bfloat16 [8192, 8192], P('seq', 'col'), may hold values from -0.0625 to 0.0625
Outputs:
- fine_hidden: bfloat16 [4, 4096, 1536], P('seq', 'col')
- coarse_out: bfloat16 [4, 704, 8192], P('seq', None, 'col')
The draws below stay inside these ranges and needn't reach their ends.
Inputs may be any that keep to these rules, and one draw needn't show every extreme that they name: `flags`: the first byte of every sequence starts a stretch, every sequence holds exactly 704 starts, every device's 128 bytes of a sequence hold at least one start and at most 66, and in every sequence some device holds exactly 66.
All inputs are finite; a program needn't handle non-finite values.
Results may differ from the reference program's by a relative error of at most 0.014.
Values may be sent and summed in bfloat16 or wider, within the bound.
No kernel may reach another device: no remote copies, remote signals or barrier semaphores. Data moves between devices by JAX's collectives and lax.ppermute only.
A program may use at most 128 MiB of HBM per device.

```python
import jax
import jax.numpy as jnp
from jax import lax

DF = 1536
FH = 12
DC = 8192
HEADS = 64
KVH = 8
DKV = 1024
BYTES_DEV = 128
CPD = 22
SEQS = 4
LEN = 4096
CH = 704
N_SEQ = 4
N_COL = 32


def draw_flags(key, part):
    key = jax.random.fold_in(key, 11)

    def one_sequence(seq_key):
        order_key, delta_key, score_key = jax.random.split(seq_key, 3)
        rank = jnp.arange(N_COL, dtype=jnp.int32)
        deltas = jax.random.randint(delta_key, (N_COL,), 0, CPD, dtype=jnp.int32)
        pair_index = jnp.maximum(rank - 5, 0) // 2
        sign = jnp.where((rank - 5) % 2 == 0, 1, -1).astype(jnp.int32)
        spread = CPD + sign * deltas[pair_index]
        alone = (rank == N_COL - 1) & ((N_COL - 5) % 2 == 1)
        spread = jnp.where(alone, CPD, spread)
        by_rank = jnp.where(rank == 0, 3 * CPD, jnp.where(rank <= 4, CPD // 2, spread)).astype(jnp.int32)
        order = jax.random.permutation(order_key, N_COL)
        counts = jnp.zeros((N_COL,), jnp.int32).at[order].set(by_rank)
        scores = jax.random.randint(score_key, (N_COL, BYTES_DEV), 0, 2 ** 20, dtype=jnp.int32) * BYTES_DEV
        scores = scores + jnp.arange(BYTES_DEV, dtype=jnp.int32)[None, :]
        scores = scores.at[0, 0].set(2 ** 30)
        ranks = jnp.argsort(jnp.argsort(-scores, axis=1), axis=1)
        return (ranks < counts[:, None]).astype(jnp.int32).reshape(N_COL * BYTES_DEV)
    return jax.vmap(one_sequence)(jax.random.split(key, N_SEQ))


def draw_fine_qkv(key, part):
    key = jax.random.fold_in(key, 21)
    base_key = jax.random.fold_in(key, 0)
    scale = DF ** (-0.5)
    base = jax.random.truncated_normal(base_key, -5.0, 5.0, (DF, 3, DF), jnp.float32) * scale
    return base.astype(jnp.bfloat16)


def draw_kv_weight(key, part):
    key = jax.random.fold_in(key, 31)
    key_part, value_part = jax.random.split(key)
    scale = DC ** (-0.5)
    keys = jax.random.truncated_normal(key_part, -5.0, 5.0, (DC, DKV), jnp.float32) * scale
    values = jax.random.truncated_normal(value_part, -5.0, 5.0, (DC, DKV), jnp.float32) * scale
    return jnp.stack([keys, values], axis=1).astype(jnp.bfloat16)


def draw_q_weight(key, part):
    key = jax.random.fold_in(key, 41)
    own_key = jax.random.fold_in(key, 0)
    own = jax.random.truncated_normal(own_key, -5.0, 5.0, (DC, DC), jnp.float32) * DC ** (-0.5)
    return own.astype(jnp.bfloat16)


def steps_of(rng, extent, shards, smallest, largest):
    def one(position, shards_of):
        steps = jax.random.uniform(jax.random.fold_in(jax.random.fold_in(rng, 6), position), (shards_of,), jnp.float32, smallest / len(shards), largest / len(shards))
        return jnp.repeat(jnp.exp(steps), extent[position] // shards_of).reshape((-1,) + (1,) * (len(extent) - position - 1))

    level = one(*shards[0])
    for cut in shards[1:]:
        level = level * one(*cut)
    return level


def normal_values(key, extent, scale, limit, cuts=(), held_as=jnp.bfloat16):
    result = scale * jax.random.normal(key, extent, jnp.float32)
    if cuts:
        result = result * steps_of(key, extent, cuts, -0.22, 0.18)
    return jnp.clip(result, -limit, limit).astype(held_as)


def setup_inputs(seed: int = 0) -> dict:
    key_of = jax.random.split(jax.random.key(seed), 11)
    return {
        "byte_in": normal_values(key_of[0], (SEQS, LEN, DF), 1.0, 6.0, ((0, 4), (1, 32))),
        "flags": draw_flags(jax.random.fold_in(key_of[10], 71), 0),
        "fine_gain": jnp.clip(1.0 + 0.1 * jax.random.normal(key_of[2], (DF,), jnp.float32), 0.5, 1.5),
        "fine_qkv": draw_fine_qkv(jax.random.fold_in(key_of[10], 71), 0),
        "fine_out": normal_values(key_of[4], (DF, DF), DF ** -0.5, 0.15625),
        "up_weight": normal_values(key_of[5], (DF, DC), DF ** -0.5, 0.15625, ((0, 4), (1, 32))),
        "coarse_gain": jnp.clip(1.0 + 0.1 * jax.random.normal(key_of[6], (DC,), jnp.float32), 0.5, 1.5),
        "q_weight": draw_q_weight(jax.random.fold_in(key_of[10], 71), 0),
        "kv_weight": draw_kv_weight(jax.random.fold_in(key_of[10], 71), 0),
        "out_weight": normal_values(key_of[9], (DC, DC), DC ** -0.5, 0.0625, ((0, 4), (1, 32))),
    }


eps = 1e-05
neg_fill = -1e+30

def rms_scale(values, gain):
    mean_sq = lax.optimization_barrier(jnp.mean(values * values, axis=-1, keepdims=True))
    return values * lax.rsqrt(mean_sq + eps) * gain

def softmax_rows(scores, valid):
    masked = jnp.where(valid, scores, neg_fill)
    top = lax.optimization_barrier(jnp.max(masked, axis=-1, keepdims=True))
    expo = jnp.exp(masked - top)
    return expo / lax.optimization_barrier(jnp.sum(expo, axis=-1, keepdims=True))

def fine_layer(byte_row, fine_gain, fine_qkv, fine_out):
    head_fine = DF // FH
    length = byte_row.shape[0]
    normed = rms_scale(byte_row.astype(jnp.float32), fine_gain).astype(jnp.bfloat16)
    proj = jnp.dot(normed, fine_qkv.reshape(DF, 3 * DF), preferred_element_type=jnp.float32).astype(jnp.bfloat16)
    proj = proj.reshape(length, 3, FH, head_fine)
    queries = proj[:, 0]
    pairs = jnp.concatenate([jnp.zeros((BYTES_DEV, 2, FH, head_fine), jnp.bfloat16), proj[:, 1:]], axis=0)
    query_index = jnp.arange(BYTES_DEV, dtype=jnp.int32)[:, None]
    key_index = jnp.arange(2 * BYTES_DEV, dtype=jnp.int32)[None, :]

    def block(index):
        start = index * BYTES_DEV
        block_q = lax.dynamic_slice_in_dim(queries, start, BYTES_DEV, 0).astype(jnp.float32)
        block_kv = lax.dynamic_slice_in_dim(pairs, start, 2 * BYTES_DEV, 0).astype(jnp.float32)
        scores = jnp.einsum('qhd,khd->hqk', block_q, block_kv[:, 0]) * head_fine ** (-0.5)
        valid = (key_index > query_index) & (key_index <= query_index + BYTES_DEV) & (key_index + start >= BYTES_DEV)
        weights = softmax_rows(scores, valid[None]).astype(jnp.bfloat16)
        mix = jnp.einsum('hqk,khd->qhd', weights.astype(jnp.float32), block_kv[:, 1])
        return mix.astype(jnp.bfloat16)
    mixed = lax.map(block, jnp.arange(length // BYTES_DEV, dtype=jnp.int32)).reshape(length, DF)
    branch = jnp.dot(mixed, fine_out, preferred_element_type=jnp.float32)
    return (byte_row.astype(jnp.float32) + branch).astype(jnp.bfloat16)

def coarse_layer(pooled, up_weight, coarse_gain, q_weight, kv_weight, out_weight):
    head_coarse = DC // HEADS
    group = HEADS // KVH
    count = pooled.shape[0]
    coarse_in = jnp.dot(pooled, up_weight, preferred_element_type=jnp.float32).astype(jnp.bfloat16)
    normed = rms_scale(coarse_in.astype(jnp.float32), coarse_gain).astype(jnp.bfloat16)
    queries = jnp.dot(normed, q_weight, preferred_element_type=jnp.float32).astype(jnp.bfloat16)
    queries = queries.reshape(count, KVH, group, head_coarse)
    pairs = jnp.dot(normed, kv_weight.reshape(DC, 2 * DKV), preferred_element_type=jnp.float32).astype(jnp.bfloat16)
    pairs = pairs.reshape(count, 2, KVH, head_coarse)
    scores = jnp.einsum('qkgd,skd->kgqs', queries.astype(jnp.float32), pairs[:, 0].astype(jnp.float32)) * head_coarse ** (-0.5)
    rows = jnp.arange(count, dtype=jnp.int32)
    causal = rows[:, None] >= rows[None, :]
    weights = softmax_rows(scores, causal).astype(jnp.bfloat16)
    mix = jnp.einsum('kgqs,skd->qkgd', weights.astype(jnp.float32), pairs[:, 1].astype(jnp.float32))
    mix = mix.astype(jnp.bfloat16).reshape(count, DC)
    branch = jnp.dot(mix, out_weight, preferred_element_type=jnp.float32)
    return (coarse_in.astype(jnp.float32) + branch).astype(jnp.bfloat16)

def reference(byte_in, flags, fine_gain, fine_qkv, fine_out, up_weight, coarse_gain, q_weight, kv_weight, out_weight):

    def one_sequence(rows):
        byte_row, flag_row = rows
        fine_hidden = fine_layer(byte_row, fine_gain, fine_qkv, fine_out)
        ids = (jnp.cumsum(flag_row) - 1).astype(jnp.int32)
        sums = jax.ops.segment_sum(fine_hidden.astype(jnp.float32), ids, num_segments=CH)
        lens = jax.ops.segment_sum(jnp.ones(ids.shape, jnp.float32), ids, num_segments=CH)
        pooled = (sums / lens[:, None]).astype(jnp.bfloat16)
        coarse_out = coarse_layer(pooled, up_weight, coarse_gain, q_weight, kv_weight, out_weight)
        return (fine_hidden, coarse_out)
    fine_all, coarse_all = lax.map(one_sequence, (byte_in, flags))
    return (fine_all, coarse_all)
```

```python
import jax
import jax.numpy as jnp
import numpy as np
from jax import lax
from jax.sharding import Mesh, PartitionSpec as P

DF = 1536
FH = 12
DC = 8192
HEADS = 64
KVH = 8
CPD = 22
MAXC = 66
SLOTS = 72
AXES = ("x", "z", "y", "core")
SIZES = (4, 4, 4, 2)

eps = 1e-05
neg_fill = -1e30
bf16 = jnp.bfloat16
f32 = jnp.float32


def send(value, target):
    pairs = []
    for source in range(128):
        where = tuple(int(i) for i in np.unravel_index(source, SIZES))
        goal = tuple(int(i) % n for i, n in zip(target(*where), SIZES))
        pairs.append((source, int(np.ravel_multi_index(goal, SIZES))))
    return lax.ppermute(value, AXES, pairs)


def swap_core(value):
    return send(value, lambda x, z, y, k: (x, z, y, 1 - k))


def along_x(value, d):
    return send(value, lambda x, z, y, k: (x + d, z, y, k))


def along_y(value, d):
    return send(value, lambda x, z, y, k: (x, z, y + d, k))


def along_z(value, d):
    return send(value, lambda x, z, y, k: (x, z + d, y, k))


def first_leg(value, d):
    return send(value, lambda x, z, y, k: (x, z, y + d, k) if k == 0 else (x, z + d, y, k))


def second_leg(value, d):
    return send(value, lambda x, z, y, k: (x, z + d, y, k) if k == 0 else (x, z, y + d, k))


def ordered(own, arrived, index):
    out = jnp.zeros((4,) + own.shape, own.dtype)
    out = lax.dynamic_update_index_in_dim(out, own, index, 0)
    for d, block in enumerate(arrived, 1):
        out = lax.dynamic_update_index_in_dim(out, block, (index - d) % 4, 0)
    return out


def gather4(value, move, index):
    return ordered(value, [move(value, d) for d in (1, 2, 3)], index)


def by_core(mine, other, core):
    return jnp.where(core == 0, jnp.stack([mine, other]), jnp.stack([other, mine]))


def gather_col(halves, core, first_index, second_index):
    mine = lax.dynamic_index_in_dim(halves, core, 0, keepdims=False)
    other = lax.dynamic_index_in_dim(halves, 1 - core, 0, keepdims=False)
    pair = by_core(mine, swap_core(other), core)
    row = gather4(pair, first_leg, first_index)
    return gather4(row, second_leg, second_index)


def rms_scale(values, gain):
    mean_sq = jnp.mean(values * values, axis=-1, keepdims=True)
    return values * lax.rsqrt(mean_sq + eps) * gain


def softmax_rows(scores, valid):
    masked = jnp.where(valid, scores, neg_fill)
    top = jnp.max(masked, axis=-1, keepdims=True)
    expo = jnp.exp(masked - top)
    return expo / jnp.sum(expo, axis=-1, keepdims=True)


def dot(a, b):
    return jnp.dot(a, b, preferred_element_type=f32)


def fine_layer(byte_in, earlier, fine_gain, fine_qkv, fine_out, position):
    span = byte_in.shape[0]
    head = DF // FH
    both = jnp.concatenate([earlier, byte_in], axis=0)
    normed = rms_scale(both.astype(f32), fine_gain).astype(bf16)
    proj = dot(normed, fine_qkv.reshape(DF, 3 * DF)).astype(bf16)
    queries = proj[span:, :DF].reshape(span, FH, head)
    keys = proj[:, DF : 2 * DF].reshape(2 * span, FH, head)
    values = proj[:, 2 * DF :].reshape(2 * span, FH, head)
    scores = jnp.einsum("qhd,khd->hqk", queries, keys, preferred_element_type=f32) * head ** (-0.5)
    query_index = jnp.arange(span, dtype=jnp.int32)[:, None]
    key_index = jnp.arange(2 * span, dtype=jnp.int32)[None, :]
    valid = (
        (key_index > query_index)
        & (key_index <= query_index + span)
        & (key_index + position * span >= span)
    )
    weights = softmax_rows(scores, valid[None]).astype(bf16)
    mixed = jnp.einsum("hqk,khd->qhd", weights, values, preferred_element_type=f32)
    mixed = mixed.astype(bf16).reshape(span, DF)
    return (byte_in.astype(f32) + dot(mixed, fine_out)).astype(bf16)


def body(
    byte_in,
    flags,
    fine_gain,
    fine_qkv,
    fine_out,
    up_weight,
    coarse_gain,
    q_weight,
    kv_weight,
    out_weight,
):
    x, z, y, core = (lax.axis_index(name) for name in AXES)
    position = z * 8 + y * 2 + core
    first_index = jnp.where(core == 0, y, z)
    second_index = jnp.where(core == 0, z, y)
    columns = 32
    stretches = CPD * columns
    half = stretches // 2
    span = byte_in.shape[1]
    embedded = byte_in[0]

    def following(x, z, y, k):
        c = (z * 8 + y * 2 + k + 1) % 32
        return (x, c // 8, c // 2 % 4, c % 2)

    earlier = send(embedded, following)

    flag_row = flags[0]
    local = jnp.cumsum(flag_row) - 1
    count = jnp.sum(flag_row)
    head_len = jnp.sum((local < 0).astype(jnp.int32))
    last_len = jnp.sum((local == count - 1).astype(jnp.int32))
    lane = jnp.arange(128, dtype=jnp.int32)[None, :]
    facts = jnp.where(lane == 0, count, jnp.where(lane == 1, head_len, last_len))
    all_facts = gather_col(jnp.stack([facts, facts]), core, first_index, second_index)
    all_facts = all_facts.reshape(4, 4, 2, 128)[..., :3]
    all_facts = jnp.where(core == 0, all_facts, jnp.swapaxes(all_facts, 0, 1)).reshape(columns, 3)
    counts = all_facts[:, 0]
    ends = jnp.cumsum(counts)
    begins = ends - counts
    next_head = jnp.concatenate([all_facts[1:, 1], jnp.zeros((1,), jnp.int32)])
    whole_last = all_facts[:, 2] + next_head

    turned = send(up_weight, lambda x, z, y, k: (z, x, y, k))
    up_block = gather_col(turned.reshape(2, 192, 256), core, first_index, second_index)
    up_block = jnp.where(core == 0, up_block, jnp.swapaxes(up_block, 0, 1))
    up_block = up_block.transpose(0, 3, 1, 2, 4).reshape(768, 2048)
    gain_block = lax.dynamic_slice_in_dim(coarse_gain, x * 2048, 2048, 0)
    up_block = (up_block.astype(f32) * gain_block).astype(bf16)
    qkv_own = jnp.concatenate([q_weight, kv_weight.reshape(2048, 64)], axis=1)
    qkv_other = swap_core(qkv_own)
    first = jnp.where(core == 0, qkv_own, qkv_other)
    second = jnp.where(core == 0, qkv_other, qkv_own)
    qkv_pair = jnp.concatenate([first[:, :256], second[:, :256], first[:, 256:], second[:, 256:]], axis=1)
    folded = dot(up_block, qkv_pair).reshape(4, 192, 640)
    total = lax.dynamic_index_in_dim(folded, x, 0, keepdims=False)
    rounded = folded.astype(bf16)
    for d in (1, 2, 3):
        piece = lax.dynamic_index_in_dim(rounded, (x + d) % 4, 0, keepdims=False)
        total = total + along_x(piece, d).astype(f32)
    folded = gather4(total.astype(bf16), along_x, x).reshape(768, 640)
    q_first, q_second, kv_pair = folded[:, :256], folded[:, 256:512], folded[:, 512:]
    give = jnp.concatenate([jnp.where(core == 0, q_second, q_first), kv_pair], axis=1)
    keep = jnp.concatenate([jnp.where(core == 0, q_first, q_second), kv_pair], axis=1)
    folded = jnp.stack([keep, swap_core(give)])
    kv_near = folded[:, :, 256:]
    kv_far = send(kv_near, lambda x, z, y, k: (x, z, y ^ 1, k))
    kv_all = jnp.where(
        y % 2 == 0, jnp.stack([kv_near, kv_far], axis=2), jnp.stack([kv_far, kv_near], axis=2)
    )
    kv_all = kv_all.reshape(2, 768, 4, 2, 32).transpose(0, 1, 3, 2, 4).reshape(2, 768, 256)
    up_cols = gather4(up_weight, along_x, x).reshape(4, 2, 192, 256)
    up_cols = up_cols.transpose(1, 0, 2, 3).reshape(2, 768, 256)
    up_cols = jnp.where(core == 0, up_cols, up_cols[::-1])
    weights_all = jnp.concatenate([up_cols, folded[:, :, :256], kv_all], axis=2)

    out_turned = send(out_weight, lambda x, z, y, k: (z, x, y, k))
    out_mine = gather4(out_turned, along_x, x)
    out_pair = by_core(out_mine, swap_core(out_mine), core)
    out_block = out_pair.transpose(2, 1, 0, 3).reshape(2048, 2048)

    fine_hidden = fine_layer(embedded, earlier, fine_gain, fine_qkv, fine_out, position)

    slot_index = jnp.arange(SLOTS, dtype=jnp.int32)
    before = jnp.where(position == 0, 0, (position - 1) % columns)
    before_len = lax.dynamic_index_in_dim(whole_last, before, 0, keepdims=False)
    last_whole = lax.dynamic_index_in_dim(whole_last, position, 0, keepdims=False)
    slot_of = jnp.where(local < 0, MAXC, local)
    slot_table = slot_of[None, :] == slot_index[:, None]
    lens = jnp.sum(slot_table.astype(jnp.int32), axis=1)
    lens = jnp.where(slot_index == MAXC, before_len, jnp.where(slot_index == count - 1, last_whole, lens))
    inverse = 1.0 / jnp.maximum(lens, 1).astype(f32)
    slots = (dot(slot_table.astype(bf16), fine_hidden) * inverse[:, None]).astype(bf16)
    slots = slots.reshape(SLOTS, 4, 2, 192).transpose(2, 0, 1, 3).reshape(2, SLOTS, 768)
    all_slots = gather_col(slots, core, first_index, second_index).reshape(columns * SLOTS, 768)

    outer = jnp.arange(4, dtype=jnp.int32)[:, None, None, None]
    inner = jnp.arange(4, dtype=jnp.int32)[None, :, None, None]
    pair_core = jnp.arange(2, dtype=jnp.int32)[None, None, :, None]
    begin_grid = begins.reshape(4, 4, 2)
    count_grid = counts.reshape(4, 4, 2)
    begin_grid = jnp.where(core == 0, begin_grid, jnp.swapaxes(begin_grid, 0, 1))[..., None]
    count_grid = jnp.where(core == 0, count_grid, jnp.swapaxes(count_grid, 0, 1))[..., None]
    place = jnp.where(
        slot_index == MAXC,
        begin_grid - 1,
        jnp.where(slot_index < count_grid, begin_grid + slot_index, -1),
    ).reshape(1, columns * SLOTS)
    choose = (place == jnp.arange(stretches, dtype=jnp.int32)[:, None]).astype(bf16)
    pooled = dot(choose, all_slots).astype(bf16)
    pooled_other = swap_core(pooled)

    up_out = dot(pooled, weights_all[0, :, :256]) + dot(pooled_other, weights_all[1, :, :256])
    coarse_in = up_out.astype(bf16)
    coarse_f32 = coarse_in.astype(f32)
    squares = jnp.sum(coarse_f32 * coarse_f32, axis=1).reshape(1, stretches)
    squares = squares + swap_core(squares)
    for flip in (1, 2):
        squares = squares + send(squares, lambda x, z, y, k: (x, z, y ^ flip, k))
    for flip in (1, 2):
        squares = squares + send(squares, lambda x, z, y, k: (x, z ^ flip, y, k))
    scale = lax.rsqrt(squares / DC + eps).reshape(stretches, 1)
    qkv = dot(pooled, weights_all[0, :, 256:]) + dot(pooled_other, weights_all[1, :, 256:])
    qkv = (qkv * scale).astype(bf16)
    head = DC // HEADS
    queries = qkv[:, :256].reshape(stretches, 2, head)
    keys = qkv[:, 256 : 256 + head]
    values = qkv[:, 256 + head :]
    scores = jnp.einsum("qhd,kd->hqk", queries, keys, preferred_element_type=f32) * head ** (-0.5)
    rows = jnp.arange(stretches, dtype=jnp.int32)
    causal = rows[:, None] >= rows[None, :]
    coarse_weights = softmax_rows(scores, causal).astype(bf16)
    mix = jnp.einsum("hqk,kd->qhd", coarse_weights, values, preferred_element_type=f32)
    mix = mix.astype(bf16).reshape(2, half, 256)

    mine = lax.dynamic_index_in_dim(mix, core, 0, keepdims=False)
    other = lax.dynamic_index_in_dim(mix, 1 - core, 0, keepdims=False)
    got = swap_core(other)
    pair = jnp.where(
        core == 0, jnp.concatenate([mine, got], axis=1), jnp.concatenate([got, mine], axis=1)
    )
    group = jnp.zeros((half, 2048), bf16)
    group = lax.dynamic_update_slice(group, pair, (0, y * 512))
    for d in (1, 2, 3):
        group = lax.dynamic_update_slice(group, along_y(pair, d), (0, (y - d) % 4 * 512))
    partial = dot(group, out_block)
    branch = lax.dynamic_slice(partial, (0, z * 512), (half, 512))
    for d in (1, 2, 3):
        piece = lax.dynamic_slice(partial, (0, (z + d) % 4 * 512), (half, 512)).astype(bf16)
        branch = branch + along_z(piece, d).astype(f32)
    branch_mine = lax.dynamic_slice(branch, (0, core * 256), (half, 256))
    branch_other = lax.dynamic_slice(branch, (0, (1 - core) * 256), (half, 256)).astype(bf16)
    branch_other = swap_core(branch_other).astype(f32)
    branch = by_core(branch_mine, branch_other, core).reshape(stretches, 256)
    coarse_out = (coarse_f32 + branch).astype(bf16)
    return (fine_hidden.reshape(1, span, DF), coarse_out.reshape(1, stretches, 256))


def solution(mesh):
    grid = Mesh(mesh.devices.reshape(SIZES), AXES)
    col = ("z", "y", "core")
    in_specs = (
        P("x", col, None),
        P("x", col),
        P(),
        P(),
        P(),
        P("x", col),
        P(),
        P("x", col),
        P("x", None, col),
        P("x", col),
    )
    out_specs = (P("x", col, None), P("x", None, col))
    return jax.shard_map(body, mesh=grid, in_specs=in_specs, out_specs=out_specs, check_vma=False)
```

```python
import jax
import jax.numpy as jnp
import numpy as np
from jax import lax
from jax.sharding import Mesh, PartitionSpec as P

DF = 1536
FH = 12
DC = 8192
HEADS = 64
KVH = 8
CPD = 22
MAXC = 66
SLOTS = 72
SLOTS_UP = 72
AXES = ("x", "z", "y", "core")
SIZES = (4, 4, 4, 2)

eps = 1e-05
neg_fill = -1e30
bf16 = jnp.bfloat16
f32 = jnp.float32


def send(value, target):
    pairs = []
    for source in range(128):
        where = tuple(int(i) for i in np.unravel_index(source, SIZES))
        goal = tuple(int(i) % n for i, n in zip(target(*where), SIZES))
        pairs.append((source, int(np.ravel_multi_index(goal, SIZES))))
    return lax.ppermute(value, AXES, pairs)


def swap_core(value):
    return send(value, lambda x, z, y, k: (x, z, y, 1 - k))


def along_x(value, d):
    return send(value, lambda x, z, y, k: (x + d, z, y, k))


def along_y(value, d):
    return send(value, lambda x, z, y, k: (x, z, y + d, k))


def along_z(value, d):
    return send(value, lambda x, z, y, k: (x, z + d, y, k))


def first_leg(value, d):
    return send(value, lambda x, z, y, k: (x, z, y + d, k) if k == 0 else (x, z + d, y, k))


def second_leg(value, d):
    return send(value, lambda x, z, y, k: (x, z + d, y, k) if k == 0 else (x, z, y + d, k))


def gather4(value, move, index):
    out = jnp.zeros((4,) + value.shape, value.dtype)
    out = lax.dynamic_update_index_in_dim(out, value, index, 0)
    for d in (1, 2, 3):
        out = lax.dynamic_update_index_in_dim(out, move(value, d), (index - d) % 4, 0)
    return out


def gather_back(value, move):
    return jnp.stack([value] + [move(value, d) for d in (1, 2, 3)])


def softmax_rows(scores, valid):
    masked = jnp.where(valid, scores, neg_fill)
    top = jnp.max(masked, axis=-1, keepdims=True)
    expo = jnp.exp(masked - top)
    return expo / jnp.sum(expo, axis=-1, keepdims=True)


def dot(a, b):
    return jnp.dot(a, b, preferred_element_type=f32)


def dot_t(a, b):
    return lax.dot_general(a, b, (((1,), (1,)), ((), ())), preferred_element_type=f32)


def rms_scale(values, gain):
    mean_sq = jnp.mean(values * values, axis=-1, keepdims=True)
    return values * lax.rsqrt(mean_sq + eps) * gain


def fine_layer(position, earlier, own, gain, qkv, out, table, inverse):
    span = own.shape[0]
    both = jnp.concatenate([earlier, own], axis=0)
    normed = rms_scale(both.astype(f32), gain).astype(bf16)
    queries = dot(normed[span:], qkv[0]).astype(bf16).reshape(span, FH, 128)
    keys = dot(normed, qkv[1]).astype(bf16).reshape(2 * span, FH, 128)
    values = dot(normed, qkv[2]).astype(bf16).reshape(2 * span, FH, 128)
    scores = jnp.einsum("qhd,khd->hqk", queries, keys, preferred_element_type=f32) * 128 ** (-0.5)
    query_index = jnp.arange(span, dtype=jnp.int32)[:, None]
    key_index = jnp.arange(2 * span, dtype=jnp.int32)[None, :]
    valid = (
        (key_index > query_index)
        & (key_index <= query_index + span)
        & (key_index + position * span >= span)
    )
    weights = softmax_rows(scores, valid[None]).astype(bf16)
    mixed = jnp.einsum("hqk,khd->qhd", weights, values, preferred_element_type=f32)
    mixed = mixed.astype(bf16).reshape(span, DF)
    hidden = (own.astype(f32) + dot(mixed, out)).astype(bf16)
    slots = (dot(table, hidden) * inverse).astype(bf16)
    return hidden, jnp.stack([slots[:, :768], slots[:, 768:]])


def fold(core, up, gain, q_mine, q_other, kv):
    rows = []
    for row in range(2):
        blocks = []
        for y in range(4):
            for k in range(2):
                z = 2 * row + k
                blocks.append(jnp.where(core == 0, up[z, y], up[y, z]))
        rows.append(jnp.concatenate(blocks, axis=1))
    block = (jnp.concatenate(rows, axis=0).astype(f32) * gain).astype(bf16)
    return dot(block, jnp.concatenate([q_mine, q_other], axis=1)), dot_t(block, kv)


def body(
    byte_in,
    flags,
    fine_gain,
    fine_qkv,
    fine_out,
    up_weight,
    coarse_gain,
    q_weight,
    kv_weight,
    out_weight,
):
    x, z, y, core = (lax.axis_index(name) for name in AXES)
    position = z * 8 + y * 2 + core
    first_index = jnp.where(core == 0, y, z)
    second_index = jnp.where(core == 0, z, y)
    columns = 32
    stretches = CPD * columns
    half = stretches // 2
    embedded = byte_in[0]
    four = jnp.arange(4, dtype=jnp.int32)

    def following(x, z, y, k):
        c = (z * 8 + y * 2 + k + 1) % 32
        return (x, c // 8, c // 2 % 4, c % 2)

    earlier = send(embedded, following)

    turned = send(up_weight, lambda x, z, y, k: (z, 2 * (x % 2) + k, y, x // 2))

    flag_row = flags[0]
    local = jnp.cumsum(flag_row) - 1
    count = jnp.sum(flag_row)
    head_len = jnp.sum((local < 0).astype(jnp.int32))
    last_len = jnp.sum((local == count - 1).astype(jnp.int32))
    lane = jnp.arange(128, dtype=jnp.int32)[None, :]
    facts = jnp.where(lane // 32 == 0, count, jnp.where(lane // 32 == 1, head_len, last_len))
    facts = jnp.where(lane % 32 == position, facts, 0)
    facts = facts + swap_core(facts)
    for flip in (1, 2):
        facts = facts + send(facts, lambda x, z, y, k: (x, z, y ^ flip, k))
    for flip in (1, 2):
        facts = facts + send(facts, lambda x, z, y, k: (x, z ^ flip, y, k))
    facts = facts.reshape(4, columns)
    counts = facts[0]
    begins = jnp.cumsum(counts) - counts
    whole_last = facts[2] + jnp.concatenate([facts[1, 1:], jnp.zeros((1,), jnp.int32)])

    slot_index = jnp.arange(SLOTS_UP, dtype=jnp.int32)
    last_whole = jnp.sum(jnp.where(jnp.arange(columns) == position, whole_last, 0))
    before_len = jnp.sum(jnp.where(jnp.arange(columns) == position - 1, whole_last, 0))
    slot_of = jnp.where(local < 0, MAXC, local)
    slot_table = slot_of[None, :] == slot_index[:, None]
    lens = jnp.sum(slot_table.astype(jnp.int32), axis=1)
    lens = jnp.where(
        slot_index == MAXC, before_len, jnp.where(slot_index == count - 1, last_whole, lens)
    )
    inverse = (1.0 / jnp.maximum(lens, 1).astype(f32)).reshape(SLOTS_UP, 1)

    fine_hidden, slots = fine_layer(
        position,
        earlier,
        embedded,
        fine_gain.reshape(1, DF),
        jnp.transpose(fine_qkv, (1, 0, 2)),
        fine_out,
        slot_table.astype(bf16),
        inverse,
    )

    up_block = gather4(gather4(turned, first_leg, first_index), second_leg, second_index)
    gain_block = lax.dynamic_slice_in_dim(coarse_gain, x * 2048, 2048, 0)
    kv_turned = jnp.transpose(kv_weight, (1, 2, 0)).reshape(64, 2048)
    q_other = swap_core(q_weight)
    kv_both = jnp.concatenate([kv_turned, swap_core(kv_turned)], axis=0)
    folded, folded_kv = fold(core, up_block, gain_block, q_weight, q_other, kv_both)
    folded = jnp.concatenate([folded, folded_kv], axis=1).reshape(4, 192, 640)
    total = lax.dynamic_index_in_dim(folded, x, 0, keepdims=False)
    folded = folded.astype(bf16)
    for d in (1, 2, 3):
        piece = lax.dynamic_index_in_dim(folded, (x + d) % 4, 0, keepdims=False)
        total = total + along_x(piece, d).astype(f32)
    folded = gather4(total.astype(bf16), along_x, x).reshape(768, 640)
    arrived = swap_core(folded[:, 256:])
    q_cols = jnp.stack([folded[:, :256], arrived[:, :256]])
    kv_mine = jnp.stack([folded[:, 512:576], arrived[:, 320:]])
    kv_other = jnp.stack([folded[:, 576:], arrived[:, 256:320]])
    kv_near = jnp.where(
        core == 0,
        jnp.concatenate([kv_mine, kv_other], axis=2),
        jnp.concatenate([kv_other, kv_mine], axis=2),
    )
    kv_far = send(kv_near, lambda x, z, y, k: (x, z, y ^ 1, k))
    kv_all = jnp.where(
        y % 2 == 0,
        jnp.concatenate([kv_near, kv_far], axis=2),
        jnp.concatenate([kv_far, kv_near], axis=2),
    )
    kv_all = kv_all.reshape(2, 768, 4, 2, 32).transpose(0, 1, 3, 2, 4).reshape(2, 768, 256)
    up_cols = gather4(up_weight, along_x, x).reshape(2, 768, 256)
    up_cols = jnp.where(core == 0, up_cols, up_cols[::-1])
    weights_all = jnp.concatenate([up_cols, q_cols, kv_all], axis=2)

    out_turned = send(out_weight, lambda x, z, y, k: (z, x, y, k))
    out_mine = lax.all_gather(out_turned, "x", axis=0)
    out_other = swap_core(out_mine)
    out_rows = []
    for d in range(4):
        pieces = []
        for e in range(4):
            at = ((z + e) % 4, (y - d) % 4 * 512, 0)
            own = lax.dynamic_slice(out_mine, at, (1, 512, 256))[0]
            far = lax.dynamic_slice(out_other, at, (1, 512, 256))[0]
            pieces += [own, far]
        out_rows.append(jnp.concatenate(pieces, axis=1))
    out_block = jnp.concatenate(out_rows, axis=0)

    slots = slots[:, :SLOTS]
    slot_index = slot_index[:SLOTS]
    mine = lax.dynamic_index_in_dim(slots, core, 0, keepdims=False)
    other = lax.dynamic_index_in_dim(slots, 1 - core, 0, keepdims=False)
    pair = jnp.stack([mine, swap_core(other)])
    all_slots = gather_back(gather_back(pair, first_leg), second_leg)
    all_slots = all_slots.reshape(columns * SLOTS, 768)

    first_of = (first_index - four[None, :, None]) % 4
    second_of = (second_index - four[:, None, None]) % 4
    core_of = jnp.array([0, 1], jnp.int32)[None, None, :] ^ core
    device_of = jnp.where(core == 0, second_of * 8 + first_of * 2, first_of * 8 + second_of * 2)
    device_of = (device_of + core_of).reshape(columns, 1)
    is_device = device_of == jnp.arange(columns, dtype=jnp.int32)[None, :]
    begin_of = jnp.sum(jnp.where(is_device, begins[None, :], 0), axis=1, keepdims=True)
    count_of = jnp.sum(jnp.where(is_device, counts[None, :], 0), axis=1, keepdims=True)
    place = jnp.where(
        slot_index[None, :] == MAXC,
        begin_of - 1,
        jnp.where(slot_index[None, :] < count_of, begin_of + slot_index[None, :], -1),
    ).reshape(1, columns * SLOTS)
    choose = (place == jnp.arange(stretches, dtype=jnp.int32)[:, None]).astype(bf16)
    pooled = dot(choose, all_slots).astype(bf16)
    pooled_other = swap_core(pooled)

    up_out = dot(pooled, weights_all[0, :, :256]) + dot(pooled_other, weights_all[1, :, :256])
    coarse_in = up_out.astype(bf16)
    coarse_f32 = coarse_in.astype(f32)
    squares = jnp.sum(coarse_f32 * coarse_f32, axis=1).reshape(1, stretches)
    squares = squares + swap_core(squares)
    for flip in (1, 2):
        squares = squares + send(squares, lambda x, z, y, k: (x, z, y ^ flip, k))
    for flip in (1, 2):
        squares = squares + send(squares, lambda x, z, y, k: (x, z ^ flip, y, k))
    scale = lax.rsqrt(squares / DC + eps).reshape(stretches, 1)
    qkv = dot(pooled, weights_all[0, :, 256:]) + dot(pooled_other, weights_all[1, :, 256:])
    qkv = (qkv * scale).astype(bf16)
    head = DC // HEADS
    queries = qkv[:, :256].reshape(stretches, 2, head)
    keys = qkv[:, 256 : 256 + head]
    values = qkv[:, 256 + head :]
    scores = jnp.einsum("qhd,kd->hqk", queries, keys, preferred_element_type=f32) * head ** (-0.5)
    rows = jnp.arange(stretches, dtype=jnp.int32)
    causal = rows[:, None] >= rows[None, :]
    coarse_weights = softmax_rows(scores, causal).astype(bf16)
    mix = jnp.einsum("hqk,kd->qhd", coarse_weights, values, preferred_element_type=f32)
    mix = mix.astype(bf16).reshape(2, half, 256)

    mine = lax.dynamic_index_in_dim(mix, core, 0, keepdims=False)
    other = lax.dynamic_index_in_dim(mix, 1 - core, 0, keepdims=False)
    got = swap_core(other)
    pair = jnp.where(
        core == 0, jnp.concatenate([mine, got], axis=1), jnp.concatenate([got, mine], axis=1)
    )
    group = jnp.concatenate([pair] + [along_y(pair, d) for d in (1, 2, 3)], axis=1)
    partial = dot(group, out_block)
    branch = partial[:, :512]
    for d in (1, 2, 3):
        piece = partial[:, d * 512 : (d + 1) * 512].astype(bf16)
        branch = branch + along_z(piece, d).astype(f32)
    branch_other = swap_core(branch[:, 256:].astype(bf16)).astype(f32)
    branch = jnp.where(
        core == 0,
        jnp.stack([branch[:, :256], branch_other]),
        jnp.stack([branch_other, branch[:, :256]]),
    ).reshape(stretches, 256)
    coarse_out = (coarse_f32 + branch).astype(bf16)
    return (fine_hidden.reshape(1, 128, DF), coarse_out.reshape(1, stretches, 256))


def solution(mesh):
    grid = Mesh(mesh.devices.reshape(SIZES), AXES)
    col = ("z", "y", "core")
    in_specs = (
        P("x", col, None),
        P("x", col),
        P(),
        P(),
        P(),
        P("x", col),
        P(),
        P("x", col),
        P("x", None, col),
        P("x", col),
    )
    out_specs = (P("x", col, None), P("x", None, col))
    return jax.shard_map(body, mesh=grid, in_specs=in_specs, out_specs=out_specs, check_vma=False)
```

```python
import jax
import jax.numpy as jnp
import numpy as np
from jax import lax
from jax.sharding import Mesh, PartitionSpec as P

DF = 1536
FH = 12
DC = 8192
HEADS = 64
KVH = 8
CPD = 22
MAXC = 66
SLOTS = 72
AXES = ("x", "z", "y", "core")
SIZES = (4, 4, 4, 2)

eps = 1e-05
neg_fill = -1e30
bf16 = jnp.bfloat16
f32 = jnp.float32


def send(value, target):
    pairs = []
    for source in range(128):
        where = tuple(int(i) for i in np.unravel_index(source, SIZES))
        goal = tuple(int(i) % n for i, n in zip(target(*where), SIZES))
        pairs.append((source, int(np.ravel_multi_index(goal, SIZES))))
    return lax.ppermute(value, AXES, pairs)


def swap_core(value):
    return send(value, lambda x, z, y, k: (x, z, y, 1 - k))


def along_x(value, d):
    return send(value, lambda x, z, y, k: (x + d, z, y, k))


def along_y(value, d):
    return send(value, lambda x, z, y, k: (x, z, y + d, k))


def along_z(value, d):
    return send(value, lambda x, z, y, k: (x, z + d, y, k))


def first_leg(value, d):
    return send(value, lambda x, z, y, k: (x, z, y + d, k) if k == 0 else (x, z + d, y, k))


def second_leg(value, d):
    return send(value, lambda x, z, y, k: (x, z + d, y, k) if k == 0 else (x, z, y + d, k))


def gather4(value, move, index):
    out = jnp.zeros((4,) + value.shape, value.dtype)
    out = lax.dynamic_update_index_in_dim(out, value, index, 0)
    for d in (1, 2, 3):
        out = lax.dynamic_update_index_in_dim(out, move(value, d), (index - d) % 4, 0)
    return out


def gather_back(value, move):
    return jnp.stack([value] + [move(value, d) for d in (1, 2, 3)])


def softmax_rows(scores, valid):
    masked = jnp.where(valid, scores, neg_fill)
    top = jnp.max(masked, axis=-1, keepdims=True)
    expo = jnp.exp(masked - top)
    return expo / jnp.sum(expo, axis=-1, keepdims=True)


def dot(a, b):
    return jnp.dot(a, b, preferred_element_type=f32)


def dot_t(a, b):
    return lax.dot_general(a, b, (((1,), (1,)), ((), ())), preferred_element_type=f32)


def rms_scale(values, gain):
    mean_sq = jnp.mean(values * values, axis=-1, keepdims=True)
    return values * lax.rsqrt(mean_sq + eps) * gain


def fine_normed(rows, gain):
    return rms_scale(rows.astype(f32), gain).astype(bf16)


def fine_attention(position, queries, keys, values):
    span = queries.shape[0]
    queries = queries.reshape(span, FH, 128)
    keys = keys.reshape(2 * span, FH, 128)
    values = values.reshape(2 * span, FH, 128)
    scores = jnp.einsum("qhd,khd->hqk", queries, keys, preferred_element_type=f32) * 128 ** (-0.5)
    query_index = jnp.arange(span, dtype=jnp.int32)[:, None]
    key_index = jnp.arange(2 * span, dtype=jnp.int32)[None, :]
    valid = (
        (key_index > query_index)
        & (key_index <= query_index + span)
        & (key_index + position * span >= span)
    )
    weights = softmax_rows(scores, valid[None]).astype(bf16)
    mixed = jnp.einsum("hqk,khd->qhd", weights, values, preferred_element_type=f32)
    return mixed.astype(bf16).reshape(span, DF)


def fold(core, up, gain, q_mine, q_other, kv):
    rows = []
    for row in range(2):
        blocks = []
        for y in range(4):
            for k in range(2):
                z = 2 * row + k
                blocks.append(jnp.where(core == 0, up[z, y, :384], up[y, z, :384]))
        rows.append(jnp.concatenate(blocks, axis=1))
    block = (jnp.concatenate(rows, axis=0).astype(f32) * gain).astype(bf16)
    return dot(block, jnp.concatenate([q_mine, q_other], axis=1)), dot_t(block, kv)


def body(
    byte_in,
    flags,
    fine_gain,
    fine_qkv,
    fine_out,
    up_weight,
    coarse_gain,
    q_weight,
    kv_weight,
    out_weight,
):
    x, z, y, core = (lax.axis_index(name) for name in AXES)
    position = z * 8 + y * 2 + core
    first_index = jnp.where(core == 0, y, z)
    second_index = jnp.where(core == 0, z, y)
    columns = 32
    stretches = CPD * columns
    half = stretches // 2
    embedded = byte_in[0]
    four = jnp.arange(4, dtype=jnp.int32)

    def following(x, z, y, k):
        c = (z * 8 + y * 2 + k + 1) % 32
        return (x, c // 8, c // 2 % 4, c % 2)

    earlier = send(embedded, following)

    turned = send(up_weight, lambda x, z, y, k: (z, 2 * (x % 2) + k, y, x // 2))

    flag_row = flags[0]
    local = jnp.cumsum(flag_row) - 1
    count = jnp.sum(flag_row)
    head_len = jnp.sum((local < 0).astype(jnp.int32))
    last_len = jnp.sum((local == count - 1).astype(jnp.int32))
    lane = jnp.arange(128, dtype=jnp.int32)[None, :]
    facts = jnp.where(lane == 0, count, jnp.where(lane == 1, head_len, last_len)).astype(bf16)
    facts = jnp.broadcast_to(facts, (16, 128))
    facts_other = swap_core(facts)
    kv_turned = jnp.transpose(kv_weight, (1, 2, 0)).reshape(64, 2048)
    q_other = swap_core(q_weight)
    kv_far_core = swap_core(kv_turned)
    out_turned = send(out_weight, lambda x, z, y, k: (z, x, y, k))

    qkv = jnp.transpose(fine_qkv, (1, 0, 2))
    normed = fine_normed(embedded, fine_gain)
    queries = dot(normed, qkv[0]).astype(bf16)
    turned, facts_other, queries, earlier = lax.optimization_barrier(
        (turned, facts_other, queries, earlier)
    )

    payload = jnp.concatenate([turned, jnp.concatenate([facts, facts_other], axis=1)], axis=0)
    up_row = gather4(payload, first_leg, first_index)
    both = jnp.concatenate([fine_normed(earlier, fine_gain), normed], axis=0)
    keys = dot(both, qkv[1]).astype(bf16)
    values = dot(both, qkv[2]).astype(bf16)
    up_row, keys, values, out_turned, up_weight = lax.optimization_barrier(
        (up_row, keys, values, out_turned, up_weight)
    )

    out_mine = lax.all_gather(out_turned, "x", axis=0)
    up_block = gather4(up_row, second_leg, second_index)
    mixed = fine_attention(position, queries, keys, values)
    hidden = (embedded.astype(f32) + dot(mixed, fine_out)).astype(bf16)
    up_block, hidden, q_other, kv_far_core = lax.optimization_barrier(
        (up_block, hidden, q_other, kv_far_core)
    )

    facts = up_block[:, :, 384, :].reshape(4, 4, 2, 128)[..., :3].astype(jnp.int32)
    facts = jnp.where(core == 0, facts, jnp.swapaxes(facts, 0, 1))
    facts = jnp.where(core == 0, facts, facts[:, :, ::-1]).reshape(columns, 3)
    counts = facts[:, 0]
    begins = jnp.cumsum(counts) - counts
    whole_last = facts[:, 2] + jnp.concatenate([facts[1:, 1], jnp.zeros((1,), jnp.int32)])

    slot_index = jnp.arange(SLOTS, dtype=jnp.int32)
    slot_of = jnp.where(local < 0, MAXC, local)
    slot_table = slot_of[None, :] == slot_index[:, None]
    lens = jnp.sum(slot_table.astype(jnp.int32), axis=1)
    as_sum = (slot_index == MAXC) | (slot_index == count - 1)
    inverse = jnp.where(as_sum, 1.0, 1.0 / jnp.maximum(lens, 1).astype(f32)).reshape(SLOTS, 1)
    slots = (dot(slot_table.astype(bf16), hidden) * inverse).astype(bf16)
    slots = jnp.stack([slots[:, :768], slots[:, 768:]])

    gain_block = lax.dynamic_slice_in_dim(coarse_gain, x * 2048, 2048, 0)
    kv_both = jnp.concatenate([kv_turned, kv_far_core], axis=0)
    folded, folded_kv = fold(core, up_block, gain_block, q_weight, q_other, kv_both)
    folded = jnp.concatenate([folded, folded_kv], axis=1).reshape(4, 192, 640)
    total = lax.dynamic_index_in_dim(folded, x, 0, keepdims=False)
    folded = folded.astype(bf16)
    for d in (1, 2, 3):
        piece = lax.dynamic_index_in_dim(folded, (x + d) % 4, 0, keepdims=False)
        total = total + along_x(piece, d).astype(f32)
    folded = gather4(total.astype(bf16), along_x, x).reshape(768, 640)
    arrived = swap_core(folded[:, 256:])
    q_cols = jnp.stack([folded[:, :256], arrived[:, :256]])
    kv_mine = jnp.stack([folded[:, 512:576], arrived[:, 320:]])
    kv_other = jnp.stack([folded[:, 576:], arrived[:, 256:320]])
    kv_near = jnp.where(
        core == 0,
        jnp.concatenate([kv_mine, kv_other], axis=2),
        jnp.concatenate([kv_other, kv_mine], axis=2),
    )
    kv_far = send(kv_near, lambda x, z, y, k: (x, z, y ^ 1, k))
    kv_all = jnp.where(
        y % 2 == 0,
        jnp.concatenate([kv_near, kv_far], axis=2),
        jnp.concatenate([kv_far, kv_near], axis=2),
    )
    kv_all = kv_all.reshape(2, 768, 4, 2, 32).transpose(0, 1, 3, 2, 4).reshape(2, 768, 256)
    up_cols = gather4(up_weight, along_x, x).reshape(2, 768, 256)
    up_cols = jnp.where(core == 0, up_cols, up_cols[::-1])
    weights_all = jnp.concatenate([up_cols, q_cols, kv_all], axis=2)

    out_other = swap_core(out_mine)
    out_rows = []
    for d in range(4):
        pieces = []
        for e in range(4):
            at = ((z + e) % 4, (y - d) % 4 * 512, 0)
            own = lax.dynamic_slice(out_mine, at, (1, 512, 256))[0]
            far = lax.dynamic_slice(out_other, at, (1, 512, 256))[0]
            pieces += [own, far]
        out_rows.append(jnp.concatenate(pieces, axis=1))
    out_block = jnp.concatenate(out_rows, axis=0)

    mine = lax.dynamic_index_in_dim(slots, core, 0, keepdims=False)
    other = lax.dynamic_index_in_dim(slots, 1 - core, 0, keepdims=False)
    pair = jnp.stack([mine, swap_core(other)])
    all_slots = gather_back(gather_back(pair, first_leg), second_leg)
    all_slots = all_slots.reshape(columns * SLOTS, 768)

    first_of = (first_index - four[None, :, None]) % 4
    second_of = (second_index - four[:, None, None]) % 4
    core_of = jnp.array([0, 1], jnp.int32)[None, None, :] ^ core
    device_of = jnp.where(core == 0, second_of * 8 + first_of * 2, first_of * 8 + second_of * 2)
    device_of = (device_of + core_of).reshape(columns, 1)
    is_device = device_of == jnp.arange(columns, dtype=jnp.int32)[None, :]
    begin_of = jnp.sum(jnp.where(is_device, begins[None, :], 0), axis=1, keepdims=True)
    count_of = jnp.sum(jnp.where(is_device, counts[None, :], 0), axis=1, keepdims=True)
    place = jnp.where(
        slot_index[None, :] == MAXC,
        begin_of - 1,
        jnp.where(slot_index[None, :] < count_of, begin_of + slot_index[None, :], -1),
    ).reshape(1, columns * SLOTS)
    choose = (place == jnp.arange(stretches, dtype=jnp.int32)[:, None]).astype(bf16)
    row = jnp.arange(stretches, dtype=jnp.int32)[:, None]
    is_last = row == (begins + counts - 1)[None, :]
    row_len = jnp.sum(jnp.where(is_last, whole_last[None, :], 0), axis=1, keepdims=True)
    row_scale = 1.0 / jnp.maximum(row_len, 1).astype(f32)
    pooled = (dot(choose, all_slots) * row_scale).astype(bf16)
    pooled_other = swap_core(pooled)

    up_out = dot(pooled, weights_all[0, :, :256]) + dot(pooled_other, weights_all[1, :, :256])
    coarse_in = up_out.astype(bf16)
    coarse_f32 = coarse_in.astype(f32)
    squares = jnp.sum(coarse_f32 * coarse_f32, axis=1).reshape(1, stretches)
    squares = squares + swap_core(squares)
    squares = squares + sum(along_y(squares, d) for d in (1, 2, 3))
    squares = squares + sum(along_z(squares, d) for d in (1, 2, 3))
    scale = lax.rsqrt(squares / DC + eps).reshape(stretches, 1)
    qkv = dot(pooled, weights_all[0, :, 256:]) + dot(pooled_other, weights_all[1, :, 256:])
    qkv = (qkv * scale).astype(bf16)
    head = DC // HEADS
    queries = qkv[:, :256].reshape(stretches, 2, head)
    keys = qkv[:, 256 : 256 + head]
    values = qkv[:, 256 + head :]
    scores = jnp.einsum("qhd,kd->hqk", queries, keys, preferred_element_type=f32) * head ** (-0.5)
    rows = jnp.arange(stretches, dtype=jnp.int32)
    causal = rows[:, None] >= rows[None, :]
    coarse_weights = softmax_rows(scores, causal).astype(bf16)
    mix = jnp.einsum("hqk,kd->qhd", coarse_weights, values, preferred_element_type=f32)
    mix = mix.astype(bf16).reshape(2, half, 256)

    mine = lax.dynamic_index_in_dim(mix, core, 0, keepdims=False)
    other = lax.dynamic_index_in_dim(mix, 1 - core, 0, keepdims=False)
    got = swap_core(other)
    pair = jnp.where(
        core == 0, jnp.concatenate([mine, got], axis=1), jnp.concatenate([got, mine], axis=1)
    )
    group = jnp.concatenate([pair] + [along_y(pair, d) for d in (1, 2, 3)], axis=1)
    partial = dot(group, out_block)
    branch = partial[:, :512]
    for d in (1, 2, 3):
        piece = partial[:, d * 512 : (d + 1) * 512].astype(bf16)
        branch = branch + along_z(piece, d).astype(f32)
    branch_other = swap_core(branch[:, 256:].astype(bf16)).astype(f32)
    branch = jnp.where(
        core == 0,
        jnp.stack([branch[:, :256], branch_other]),
        jnp.stack([branch_other, branch[:, :256]]),
    ).reshape(stretches, 256)
    coarse_out = (coarse_f32 + branch).astype(bf16)
    return (hidden.reshape(1, 128, DF), coarse_out.reshape(1, stretches, 256))


def solution(mesh):
    grid = Mesh(mesh.devices.reshape(SIZES), AXES)
    col = ("z", "y", "core")
    in_specs = (
        P("x", col, None),
        P("x", col),
        P(),
        P(),
        P(),
        P("x", col),
        P(),
        P("x", col),
        P("x", None, col),
        P("x", col),
    )
    out_specs = (P("x", col, None), P("x", None, col))
    return jax.shard_map(body, mesh=grid, in_specs=in_specs, out_specs=out_specs, check_vma=False)
```

```python
import jax
import jax.numpy as jnp
import numpy as np
from jax import lax
from jax.sharding import Mesh, PartitionSpec as P

DF = 1536
FH = 12
DC = 8192
HEADS = 64
KVH = 8
CPD = 22
MAXC = 66
SLOTS = 72
AXES = ("x", "z", "y", "core")
SIZES = (4, 4, 4, 2)

eps = 1e-05
neg_fill = -1e30
bf16 = jnp.bfloat16
f32 = jnp.float32


def send(value, target):
    pairs = []
    for source in range(128):
        where = tuple(int(i) for i in np.unravel_index(source, SIZES))
        goal = tuple(int(i) % n for i, n in zip(target(*where), SIZES))
        pairs.append((source, int(np.ravel_multi_index(goal, SIZES))))
    return lax.ppermute(value, AXES, pairs)


def swap_core(value):
    return send(value, lambda x, z, y, k: (x, z, y, 1 - k))


def along_x(value, d):
    return send(value, lambda x, z, y, k: (x + d, z, y, k))


def along_y(value, d):
    return send(value, lambda x, z, y, k: (x, z, y + d, k))


def along_z(value, d):
    return send(value, lambda x, z, y, k: (x, z + d, y, k))


def first_leg(value, d):
    return send(value, lambda x, z, y, k: (x, z, y + d, k) if k == 0 else (x, z + d, y, k))


def second_leg(value, d):
    return send(value, lambda x, z, y, k: (x, z + d, y, k) if k == 0 else (x, z, y + d, k))


def gather4(value, move, index):
    out = jnp.zeros((4,) + value.shape, value.dtype)
    out = lax.dynamic_update_index_in_dim(out, value, index, 0)
    for d in (1, 2, 3):
        out = lax.dynamic_update_index_in_dim(out, move(value, d), (index - d) % 4, 0)
    return out


def gather_back(value, move):
    return jnp.stack([value] + [move(value, d) for d in (1, 2, 3)])


def softmax_rows(scores, valid):
    masked = jnp.where(valid, scores, neg_fill)
    top = jnp.max(masked, axis=-1, keepdims=True)
    expo = jnp.exp(masked - top)
    return expo / jnp.sum(expo, axis=-1, keepdims=True)


def dot(a, b):
    return jnp.dot(a, b, preferred_element_type=f32)


def dot_t(a, b):
    return lax.dot_general(a, b, (((1,), (1,)), ((), ())), preferred_element_type=f32)


def rms_scale(values, gain):
    mean_sq = jnp.mean(values * values, axis=-1, keepdims=True)
    return values * lax.rsqrt(mean_sq + eps) * gain


def fine_normed(rows, gain):
    return rms_scale(rows.astype(f32), gain).astype(bf16)


def fine_attention(position, queries, keys, values):
    span = queries.shape[0]
    queries = queries.reshape(span, FH, 128)
    keys = keys.reshape(2 * span, FH, 128)
    values = values.reshape(2 * span, FH, 128)
    scores = jnp.einsum("qhd,khd->hqk", queries, keys, preferred_element_type=f32) * 128 ** (-0.5)
    query_index = jnp.arange(span, dtype=jnp.int32)[:, None]
    key_index = jnp.arange(2 * span, dtype=jnp.int32)[None, :]
    valid = (
        (key_index > query_index)
        & (key_index <= query_index + span)
        & (key_index + position * span >= span)
    )
    weights = softmax_rows(scores, valid[None]).astype(bf16)
    mixed = jnp.einsum("hqk,khd->qhd", weights, values, preferred_element_type=f32)
    return mixed.astype(bf16).reshape(span, DF)


def fold(up, gain, q_mine, q_other, kv):
    rows = []
    for row in range(2):
        blocks = [up[2 * row + k, y, :384] for y in range(4) for k in range(2)]
        rows.append(jnp.concatenate(blocks, axis=1))
    block = (jnp.concatenate(rows, axis=0).astype(f32) * gain).astype(bf16)
    return dot(block, jnp.concatenate([q_mine, q_other], axis=1)), dot_t(block, kv)


def body(
    byte_in,
    flags,
    fine_gain,
    fine_qkv,
    fine_out,
    up_weight,
    coarse_gain,
    q_weight,
    kv_weight,
    out_weight,
):
    x, z, y, core = (lax.axis_index(name) for name in AXES)
    position = z * 8 + y * 2 + core
    first_index = jnp.where(core == 0, y, z)
    second_index = jnp.where(core == 0, z, y)
    columns = 32
    stretches = CPD * columns
    half = stretches // 2
    embedded = byte_in[0]
    four = jnp.arange(4, dtype=jnp.int32)

    def following(x, z, y, k):
        c = (z * 8 + y * 2 + k + 1) % 32
        return (x, c // 8, c // 2 % 4, c % 2)

    earlier = send(embedded, following)

    def turn(x, z, y, k):
        second = 2 * (x % 2) + k
        return (z, second, y, 0) if x < 2 else (z, y, second, 1)

    turned = send(up_weight, turn)

    flag_row = flags[0]
    local = jnp.cumsum(flag_row) - 1
    count = jnp.sum(flag_row)
    head_len = jnp.sum((local < 0).astype(jnp.int32))
    last_len = jnp.sum((local == count - 1).astype(jnp.int32))
    lane = jnp.arange(128, dtype=jnp.int32)[None, :]
    facts = jnp.where(lane == 0, count, jnp.where(lane == 1, head_len, last_len)).astype(bf16)
    facts = jnp.broadcast_to(facts, (16, 128))
    facts_other = swap_core(facts)
    kv_turned = jnp.transpose(kv_weight, (1, 2, 0)).reshape(64, 2048)
    q_other = swap_core(q_weight)
    kv_far_core = swap_core(kv_turned)

    qkv = jnp.transpose(fine_qkv, (1, 0, 2))
    normed = fine_normed(embedded, fine_gain)
    queries = dot(normed, qkv[0]).astype(bf16)
    turned, facts_other, queries, earlier, up_weight = lax.optimization_barrier(
        (turned, facts_other, queries, earlier, up_weight)
    )

    payload = jnp.concatenate([turned, jnp.concatenate([facts, facts_other], axis=1)], axis=0)
    up_row = gather4(payload, first_leg, first_index)
    up_cols = gather4(up_weight, along_x, x).reshape(2, 768, 256)
    both = jnp.concatenate([fine_normed(earlier, fine_gain), normed], axis=0)
    keys = dot(both, qkv[1]).astype(bf16)
    values = dot(both, qkv[2]).astype(bf16)
    up_row, keys, values, out_weight = lax.optimization_barrier((up_row, keys, values, out_weight))

    out_turned = send(out_weight, lambda x, z, y, k: (z, x, y, k))
    up_block = gather4(up_row, second_leg, second_index)
    mixed = fine_attention(position, queries, keys, values)
    hidden = (embedded.astype(f32) + dot(mixed, fine_out)).astype(bf16)

    slot_index = jnp.arange(SLOTS, dtype=jnp.int32)
    slot_of = jnp.where(local < 0, MAXC, local)
    slot_table = slot_of[None, :] == slot_index[:, None]
    lens = jnp.sum(slot_table.astype(jnp.int32), axis=1)
    as_sum = (slot_index == MAXC) | (slot_index == count - 1)
    inverse = jnp.where(as_sum, 1.0, 1.0 / jnp.maximum(lens, 1).astype(f32)).reshape(SLOTS, 1)
    slots = (dot(slot_table.astype(bf16), hidden) * inverse).astype(bf16)
    slots = jnp.stack([slots[:, :768], slots[:, 768:]])
    mine = lax.dynamic_index_in_dim(slots, core, 0, keepdims=False)
    other = lax.dynamic_index_in_dim(slots, 1 - core, 0, keepdims=False)
    pair = jnp.stack([mine, swap_core(other)])
    pair, up_block, q_other, kv_far_core = lax.optimization_barrier(
        (pair, up_block, q_other, kv_far_core)
    )
    slots_row = gather_back(pair, first_leg)

    facts = up_block[:, :, 384, :].reshape(4, 4, 2, 128)[..., :3].astype(jnp.int32)
    facts = jnp.where(core == 0, facts, jnp.swapaxes(facts, 0, 1))
    facts = jnp.where(core == 0, facts, facts[:, :, ::-1]).reshape(columns, 3)
    counts = facts[:, 0]
    begins = jnp.cumsum(counts) - counts
    whole_last = facts[:, 2] + jnp.concatenate([facts[1:, 1], jnp.zeros((1,), jnp.int32)])

    gain_block = lax.dynamic_slice_in_dim(coarse_gain, x * 2048, 2048, 0)
    kv_both = jnp.concatenate([kv_turned, kv_far_core], axis=0)
    folded, folded_kv = fold(up_block, gain_block, q_weight, q_other, kv_both)
    folded = jnp.concatenate([folded, folded_kv], axis=1).reshape(4, 192, 640)
    total = lax.dynamic_index_in_dim(folded, x, 0, keepdims=False)
    folded = folded.astype(bf16)
    folded, slots_row, out_turned = lax.optimization_barrier((folded, slots_row, out_turned))
    all_slots = gather_back(slots_row, second_leg)
    out_mine = lax.all_gather(out_turned, "x", axis=0)
    for d in (1, 2, 3):
        piece = lax.dynamic_index_in_dim(folded, (x + d) % 4, 0, keepdims=False)
        total = total + along_x(piece, d).astype(f32)
    folded = gather4(total.astype(bf16), along_x, x).reshape(768, 640)
    arrived = swap_core(folded[:, 256:])
    q_cols = jnp.stack([folded[:, :256], arrived[:, :256]])
    kv_mine = jnp.stack([folded[:, 512:576], arrived[:, 320:]])
    kv_other = jnp.stack([folded[:, 576:], arrived[:, 256:320]])
    kv_near = jnp.where(
        core == 0,
        jnp.concatenate([kv_mine, kv_other], axis=2),
        jnp.concatenate([kv_other, kv_mine], axis=2),
    )
    kv_far = send(kv_near, lambda x, z, y, k: (x, z, y ^ 1, k))
    kv_all = jnp.where(
        y % 2 == 0,
        jnp.concatenate([kv_near, kv_far], axis=2),
        jnp.concatenate([kv_far, kv_near], axis=2),
    )
    kv_all = kv_all.reshape(2, 768, 4, 2, 32).transpose(0, 1, 3, 2, 4).reshape(2, 768, 256)
    up_cols = jnp.where(core == 0, up_cols, up_cols[::-1])
    weights_all = jnp.concatenate([up_cols, q_cols, kv_all], axis=2)

    all_slots = all_slots.reshape(columns * SLOTS, 768)

    first_of = (first_index - four[None, :, None]) % 4
    second_of = (second_index - four[:, None, None]) % 4
    core_of = jnp.array([0, 1], jnp.int32)[None, None, :] ^ core
    device_of = jnp.where(core == 0, second_of * 8 + first_of * 2, first_of * 8 + second_of * 2)
    device_of = (device_of + core_of).reshape(columns, 1)
    is_device = device_of == jnp.arange(columns, dtype=jnp.int32)[None, :]
    begin_of = jnp.sum(jnp.where(is_device, begins[None, :], 0), axis=1, keepdims=True)
    count_of = jnp.sum(jnp.where(is_device, counts[None, :], 0), axis=1, keepdims=True)
    place = jnp.where(
        slot_index[None, :] == MAXC,
        begin_of - 1,
        jnp.where(slot_index[None, :] < count_of, begin_of + slot_index[None, :], -1),
    ).reshape(1, columns * SLOTS)
    choose = (place == jnp.arange(stretches, dtype=jnp.int32)[:, None]).astype(bf16)
    row = jnp.arange(stretches, dtype=jnp.int32)[:, None]
    is_last = row == (begins + counts - 1)[None, :]
    row_len = jnp.sum(jnp.where(is_last, whole_last[None, :], 0), axis=1, keepdims=True)
    row_scale = 1.0 / jnp.maximum(row_len, 1).astype(f32)
    pooled = (dot(choose, all_slots) * row_scale).astype(bf16)
    pooled_other = swap_core(pooled)
    pooled_other, out_mine = lax.optimization_barrier((pooled_other, out_mine))

    out_other = swap_core(out_mine)
    out_rows = []
    for d in range(4):
        pieces = []
        for e in range(4):
            at = ((z + e) % 4, (y - d) % 4 * 512, 0)
            own = lax.dynamic_slice(out_mine, at, (1, 512, 256))[0]
            far = lax.dynamic_slice(out_other, at, (1, 512, 256))[0]
            pieces += [own, far]
        out_rows.append(jnp.concatenate(pieces, axis=1))
    out_block = jnp.concatenate(out_rows, axis=0)


    up_out = dot(pooled, weights_all[0, :, :256]) + dot(pooled_other, weights_all[1, :, :256])
    coarse_in = up_out.astype(bf16)
    coarse_f32 = coarse_in.astype(f32)
    squares = jnp.sum(coarse_f32 * coarse_f32, axis=1).reshape(1, stretches)
    squares = squares + swap_core(squares)
    squares = squares + sum(along_y(squares, d) for d in (1, 2, 3))
    squares = squares + sum(along_z(squares, d) for d in (1, 2, 3))
    scale = lax.rsqrt(squares / DC + eps).reshape(stretches, 1)
    qkv = dot(pooled, weights_all[0, :, 256:]) + dot(pooled_other, weights_all[1, :, 256:])
    qkv = (qkv * scale).astype(bf16)
    head = DC // HEADS
    queries = qkv[:, :256].reshape(stretches, 2, head)
    keys = qkv[:, 256 : 256 + head]
    values = qkv[:, 256 + head :]
    scores = jnp.einsum("qhd,kd->hqk", queries, keys, preferred_element_type=f32) * head ** (-0.5)
    rows = jnp.arange(stretches, dtype=jnp.int32)
    causal = rows[:, None] >= rows[None, :]
    coarse_weights = softmax_rows(scores, causal).astype(bf16)
    mix = jnp.einsum("hqk,kd->qhd", coarse_weights, values, preferred_element_type=f32)
    mix = mix.astype(bf16).reshape(2, half, 256)

    mine = lax.dynamic_index_in_dim(mix, core, 0, keepdims=False)
    other = lax.dynamic_index_in_dim(mix, 1 - core, 0, keepdims=False)
    got = swap_core(other)
    pair = jnp.where(
        core == 0, jnp.concatenate([mine, got], axis=1), jnp.concatenate([got, mine], axis=1)
    )
    branches = []
    for part in (pair[: half // 2], pair[half // 2 :]):
        group = jnp.concatenate([part] + [along_y(part, d) for d in (1, 2, 3)], axis=1)
        partial = dot(group, out_block)
        branch = partial[:, :512]
        for d in (1, 2, 3):
            piece = partial[:, d * 512 : (d + 1) * 512].astype(bf16)
            branch = branch + along_z(piece, d).astype(f32)
        branches.append(branch)
    branch = jnp.concatenate(branches, axis=0)
    branch_other = swap_core(branch[:, 256:].astype(bf16)).astype(f32)
    branch = jnp.where(
        core == 0,
        jnp.stack([branch[:, :256], branch_other]),
        jnp.stack([branch_other, branch[:, :256]]),
    ).reshape(stretches, 256)
    coarse_out = (coarse_f32 + branch).astype(bf16)
    return (hidden.reshape(1, 128, DF), coarse_out.reshape(1, stretches, 256))


def solution(mesh):
    grid = Mesh(mesh.devices.reshape(SIZES), AXES)
    col = ("z", "y", "core")
    in_specs = (
        P("x", col, None),
        P("x", col),
        P(),
        P(),
        P(),
        P("x", col),
        P(),
        P("x", col),
        P("x", None, col),
        P("x", col),
    )
    out_specs = (P("x", col, None), P("x", None, col))
    return jax.shard_map(body, mesh=grid, in_specs=in_specs, out_specs=out_specs, check_vma=False)
```

```python
import jax
import jax.numpy as jnp
import numpy as np
from jax import lax
from jax.sharding import Mesh, PartitionSpec as P

DF = 1536
FH = 12
DC = 8192
HEADS = 64
KVH = 8
CPD = 22
MAXC = 66
SLOTS = 72
AXES = ("x", "z", "y", "core")
SIZES = (4, 4, 4, 2)

eps = 1e-05
neg_fill = -1e30
bf16 = jnp.bfloat16
f32 = jnp.float32


def send(value, target):
    pairs = []
    for source in range(128):
        where = tuple(int(i) for i in np.unravel_index(source, SIZES))
        goal = tuple(int(i) % n for i, n in zip(target(*where), SIZES))
        pairs.append((source, int(np.ravel_multi_index(goal, SIZES))))
    return lax.ppermute(value, AXES, pairs)


def swap_core(value):
    return send(value, lambda x, z, y, k: (x, z, y, 1 - k))


def along_x(value, d):
    return send(value, lambda x, z, y, k: (x + d, z, y, k))


def along_y(value, d):
    return send(value, lambda x, z, y, k: (x, z, y + d, k))


def along_z(value, d):
    return send(value, lambda x, z, y, k: (x, z + d, y, k))


def first_leg(value, d):
    return send(value, lambda x, z, y, k: (x, z, y + d, k) if k == 0 else (x, z + d, y, k))


def second_leg(value, d):
    return send(value, lambda x, z, y, k: (x, z + d, y, k) if k == 0 else (x, z, y + d, k))


def gather4(value, move, index):
    out = jnp.zeros((4,) + value.shape, value.dtype)
    out = lax.dynamic_update_index_in_dim(out, value, index, 0)
    for d in (1, 2, 3):
        out = lax.dynamic_update_index_in_dim(out, move(value, d), (index - d) % 4, 0)
    return out


def gather_back(value, move):
    return jnp.stack([value] + [move(value, d) for d in (1, 2, 3)])


def softmax_rows(scores, valid):
    masked = jnp.where(valid, scores, neg_fill)
    top = jnp.max(masked, axis=-1, keepdims=True)
    expo = jnp.exp(masked - top)
    return expo / jnp.sum(expo, axis=-1, keepdims=True)


def dot(a, b):
    return jnp.dot(a, b, preferred_element_type=f32)


def rms_scale(values, gain):
    mean_sq = jnp.mean(values * values, axis=-1, keepdims=True)
    return values * lax.rsqrt(mean_sq + eps) * gain


def fine_normed(rows, gain):
    return rms_scale(rows.astype(f32), gain).astype(bf16)


def fine_attention(position, queries, keys, values):
    span = queries.shape[0]
    queries = queries.reshape(span, FH, 128)
    keys = keys.reshape(2 * span, FH, 128)
    values = values.reshape(2 * span, FH, 128)
    scores = jnp.einsum("qhd,khd->hqk", queries, keys, preferred_element_type=f32) * 128 ** (-0.5)
    query_index = jnp.arange(span, dtype=jnp.int32)[:, None]
    key_index = jnp.arange(2 * span, dtype=jnp.int32)[None, :]
    valid = (
        (key_index > query_index)
        & (key_index <= query_index + span)
        & (key_index + position * span >= span)
    )
    weights = softmax_rows(scores, valid[None]).astype(bf16)
    mixed = jnp.einsum("hqk,khd->qhd", weights, values, preferred_element_type=f32)
    return mixed.astype(bf16).reshape(span, DF)


def fold(up, gain, weight):
    rows = []
    for row in range(2):
        blocks = [up[2 * row + k, y, :384] for y in range(4) for k in range(2)]
        rows.append(jnp.concatenate(blocks, axis=1))
    block = (jnp.concatenate(rows, axis=0).astype(f32) * gain).astype(bf16)
    return dot(block, weight).astype(bf16)


def body(
    byte_in,
    flags,
    fine_gain,
    fine_qkv,
    fine_out,
    up_weight,
    coarse_gain,
    q_weight,
    kv_weight,
    out_weight,
):
    x, z, y, core = (lax.axis_index(name) for name in AXES)
    position = z * 8 + y * 2 + core
    first_index = jnp.where(core == 0, y, z)
    second_index = jnp.where(core == 0, z, y)
    columns = 32
    stretches = CPD * columns
    half = stretches // 2
    embedded = byte_in[0]
    four = jnp.arange(4, dtype=jnp.int32)

    def following(x, z, y, k):
        c = (z * 8 + y * 2 + k + 1) % 32
        return (x, c // 8, c // 2 % 4, c % 2)

    earlier = send(embedded, following)

    def turn(x, z, y, k):
        second = 2 * (x % 2) + k
        return (z, second, y, 0) if x < 2 else (z, y, second, 1)

    turned = send(up_weight, turn)

    flag_row = flags[0]
    local = jnp.cumsum(flag_row) - 1
    count = jnp.sum(flag_row)
    head_len = jnp.sum((local < 0).astype(jnp.int32))
    last_len = jnp.sum((local == count - 1).astype(jnp.int32))
    lane = jnp.arange(128, dtype=jnp.int32)[None, :]
    facts = jnp.where(lane == 0, count, jnp.where(lane == 1, head_len, last_len)).astype(bf16)
    facts = jnp.broadcast_to(facts, (16, 128))
    facts_other = swap_core(facts)
    kv_turned = jnp.transpose(kv_weight, (1, 2, 0)).reshape(64, 2048)
    q_other = swap_core(q_weight)
    kv_far_core = swap_core(kv_turned)
    out_turned = send(out_weight, lambda x, z, y, k: (2 * x - z, x, y, k))

    qkv = jnp.transpose(fine_qkv, (1, 0, 2))
    normed = fine_normed(embedded, fine_gain)
    queries = dot(normed, qkv[0]).astype(bf16)
    turned, facts_other, queries, earlier, up_weight, q_other, kv_far_core = (
        lax.optimization_barrier(
            (turned, facts_other, queries, earlier, up_weight, q_other, kv_far_core)
        )
    )

    payload = jnp.concatenate([turned, jnp.concatenate([facts, facts_other], axis=1)], axis=0)
    up_row = gather4(payload, first_leg, first_index)
    up_cols = gather4(up_weight, along_x, x).reshape(2, 768, 256)
    both = jnp.concatenate([fine_normed(earlier, fine_gain), normed], axis=0)
    keys = dot(both, qkv[1]).astype(bf16)
    values = dot(both, qkv[2]).astype(bf16)
    up_row, keys, values, out_turned = lax.optimization_barrier((up_row, keys, values, out_turned))

    out_mine = lax.all_gather(out_turned, "x", axis=0)
    kv_both = jnp.concatenate([kv_turned, kv_far_core], axis=0).T
    qkv_weight = jnp.concatenate([q_weight, q_other, kv_both], axis=1)
    up_block = gather4(up_row, second_leg, second_index)
    mixed = fine_attention(position, queries, keys, values)
    hidden = (embedded.astype(f32) + dot(mixed, fine_out)).astype(bf16)

    slot_index = jnp.arange(SLOTS, dtype=jnp.int32)
    slot_of = jnp.where(local < 0, MAXC, local)
    slot_table = slot_of[None, :] == slot_index[:, None]
    lens = jnp.sum(slot_table.astype(jnp.int32), axis=1)
    as_sum = (slot_index == MAXC) | (slot_index == count - 1)
    inverse = jnp.where(as_sum, 1.0, 1.0 / jnp.maximum(lens, 1).astype(f32)).reshape(SLOTS, 1)
    slots = (dot(slot_table.astype(bf16), hidden) * inverse).astype(bf16)
    slots = jnp.stack([slots[:, :768], slots[:, 768:]])
    mine = lax.dynamic_index_in_dim(slots, core, 0, keepdims=False)
    other = lax.dynamic_index_in_dim(slots, 1 - core, 0, keepdims=False)
    pair = jnp.stack([mine, swap_core(other)])
    pair, up_block, qkv_weight, up_cols = lax.optimization_barrier(
        (pair, up_block, qkv_weight, up_cols)
    )
    slots_row = gather_back(pair, first_leg)

    facts = up_block[:, :, 384, :].reshape(4, 4, 2, 128)[..., :3].astype(jnp.int32)
    facts = jnp.where(core == 0, facts, jnp.swapaxes(facts, 0, 1))
    facts = jnp.where(core == 0, facts, facts[:, :, ::-1]).reshape(columns, 3)
    counts = facts[:, 0]
    begins = jnp.cumsum(counts) - counts
    whole_last = facts[:, 2] + jnp.concatenate([facts[1:, 1], jnp.zeros((1,), jnp.int32)])

    gain_block = lax.dynamic_slice_in_dim(coarse_gain, x * 2048, 2048, 0)
    folded = fold(up_block, gain_block, qkv_weight).reshape(4, 192, 640)
    folded, slots_row = lax.optimization_barrier((folded, slots_row))
    total = lax.dynamic_index_in_dim(folded, x, 0, keepdims=False).astype(f32)
    all_slots = gather_back(slots_row, second_leg)
    for d in (1, 2, 3):
        piece = lax.dynamic_index_in_dim(folded, (x + d) % 4, 0, keepdims=False)
        total = total + along_x(piece, d).astype(f32)
    folded = gather4(total.astype(bf16), along_x, x).reshape(768, 640)
    arrived = swap_core(folded[:, 256:])
    q_cols = jnp.stack([folded[:, :256], arrived[:, :256]])
    kv_mine = jnp.stack([folded[:, 512:576], arrived[:, 320:]])
    kv_other = jnp.stack([folded[:, 576:], arrived[:, 256:320]])
    kv_near = jnp.where(
        core == 0,
        jnp.concatenate([kv_mine, kv_other], axis=2),
        jnp.concatenate([kv_other, kv_mine], axis=2),
    )
    kv_far = send(kv_near, lambda x, z, y, k: (x, z, y ^ 1, k))
    kv_all = jnp.where(
        y % 2 == 0,
        jnp.concatenate([kv_near, kv_far], axis=2),
        jnp.concatenate([kv_far, kv_near], axis=2),
    )
    kv_all = kv_all.reshape(2, 768, 4, 2, 32).transpose(0, 1, 3, 2, 4).reshape(2, 768, 256)
    up_cols = jnp.where(core == 0, up_cols, up_cols[::-1])
    weights_all = jnp.concatenate([up_cols, q_cols, kv_all], axis=2)

    all_slots = all_slots.reshape(columns * SLOTS, 768)

    first_of = (first_index - four[None, :, None]) % 4
    second_of = (second_index - four[:, None, None]) % 4
    core_of = jnp.array([0, 1], jnp.int32)[None, None, :] ^ core
    device_of = jnp.where(core == 0, second_of * 8 + first_of * 2, first_of * 8 + second_of * 2)
    device_of = (device_of + core_of).reshape(columns, 1)
    is_device = device_of == jnp.arange(columns, dtype=jnp.int32)[None, :]
    begin_of = jnp.sum(jnp.where(is_device, begins[None, :], 0), axis=1, keepdims=True)
    count_of = jnp.sum(jnp.where(is_device, counts[None, :], 0), axis=1, keepdims=True)
    place = jnp.where(
        slot_index[None, :] == MAXC,
        begin_of - 1,
        jnp.where(slot_index[None, :] < count_of, begin_of + slot_index[None, :], -1),
    ).reshape(1, columns * SLOTS)
    choose = (place == jnp.arange(stretches, dtype=jnp.int32)[:, None]).astype(bf16)
    row = jnp.arange(stretches, dtype=jnp.int32)[:, None]
    is_last = row == (begins + counts - 1)[None, :]
    row_len = jnp.sum(jnp.where(is_last, whole_last[None, :], 0), axis=1, keepdims=True)
    row_scale = 1.0 / jnp.maximum(row_len, 1).astype(f32)
    pooled = (dot(choose, all_slots) * row_scale).astype(bf16)
    pooled_other = swap_core(pooled)
    pooled_other, out_mine = lax.optimization_barrier((pooled_other, out_mine))

    out_other = swap_core(out_mine)
    out_rows = []
    for d in range(4):
        pieces = []
        for e in range(4):
            at = ((z - e) % 4, (y - d) % 4 * 512, 0)
            own = lax.dynamic_slice(out_mine, at, (1, 512, 256))[0]
            far = lax.dynamic_slice(out_other, at, (1, 512, 256))[0]
            pieces += [own, far]
        out_rows.append(jnp.concatenate(pieces, axis=1))
    out_block = jnp.concatenate(out_rows, axis=0)


    up_out = dot(pooled, weights_all[0, :, :256]) + dot(pooled_other, weights_all[1, :, :256])
    coarse_in = up_out.astype(bf16)
    coarse_f32 = coarse_in.astype(f32)
    squares = jnp.sum(coarse_f32 * coarse_f32, axis=1).reshape(1, stretches)
    squares = squares + swap_core(squares)
    squares = squares + sum(along_y(squares, d) for d in (1, 2, 3))
    squares = squares + sum(along_z(squares, d) for d in (1, 2, 3))
    scale = lax.rsqrt(squares / DC + eps).reshape(stretches, 1)
    qkv = dot(pooled, weights_all[0, :, 256:]) + dot(pooled_other, weights_all[1, :, 256:])
    qkv = (qkv * scale).astype(bf16)
    head = DC // HEADS
    queries = qkv[:, :256].reshape(stretches, 2, head)
    keys = qkv[:, 256 : 256 + head]
    values = qkv[:, 256 + head :]
    scores = jnp.einsum("qhd,kd->hqk", queries, keys, preferred_element_type=f32) * head ** (-0.5)
    rows = jnp.arange(stretches, dtype=jnp.int32)
    causal = rows[:, None] >= rows[None, :]
    coarse_weights = softmax_rows(scores, causal).astype(bf16)
    mix = jnp.einsum("hqk,kd->qhd", coarse_weights, values, preferred_element_type=f32)
    mix = mix.astype(bf16).reshape(2, half, 256)

    mine = lax.dynamic_index_in_dim(mix, core, 0, keepdims=False)
    other = lax.dynamic_index_in_dim(mix, 1 - core, 0, keepdims=False)
    got = swap_core(other)
    pair = jnp.where(
        core == 0, jnp.concatenate([mine, got], axis=1), jnp.concatenate([got, mine], axis=1)
    )
    branches = []
    for part in (pair[: half // 2], pair[half // 2 :]):
        group = jnp.concatenate([part] + [along_y(part, d) for d in (1, 2, 3)], axis=1)
        partial = dot(group, out_block)
        branch = partial[:, :512]
        for d in (1, 2, 3):
            piece = partial[:, d * 512 : (d + 1) * 512].astype(bf16)
            branch = branch + along_z(piece, d).astype(f32)
        branches.append(branch)
    branch = jnp.concatenate(branches, axis=0)
    branch_other = swap_core(branch[:, 256:].astype(bf16)).astype(f32)
    branch = jnp.where(
        core == 0,
        jnp.stack([branch[:, :256], branch_other]),
        jnp.stack([branch_other, branch[:, :256]]),
    ).reshape(stretches, 256)
    coarse_out = (coarse_f32 + branch).astype(bf16)
    return (hidden.reshape(1, 128, DF), coarse_out.reshape(1, stretches, 256))


def solution(mesh):
    grid = Mesh(mesh.devices.reshape(SIZES), AXES)
    col = ("z", "y", "core")
    in_specs = (
        P("x", col, None),
        P("x", col),
        P(),
        P(),
        P(),
        P("x", col),
        P(),
        P("x", col),
        P("x", None, col),
        P("x", col),
    )
    out_specs = (P("x", col, None), P("x", None, col))
    return jax.shard_map(body, mesh=grid, in_specs=in_specs, out_specs=out_specs, check_vma=False)
```

```python
import jax
import jax.numpy as jnp
import numpy as np
from jax import lax
from jax.sharding import Mesh, PartitionSpec as P

DF = 1536
FH = 12
DC = 8192
HEADS = 64
KVH = 8
CPD = 22
MAXC = 66
SLOTS = 72
AXES = ("x", "z", "y", "core")
SIZES = (4, 4, 4, 2)

eps = 1e-05
neg_fill = -1e30
bf16 = jnp.bfloat16
f32 = jnp.float32


def send(value, target):
    pairs = []
    for source in range(128):
        where = tuple(int(i) for i in np.unravel_index(source, SIZES))
        goal = tuple(int(i) % n for i, n in zip(target(*where), SIZES))
        pairs.append((source, int(np.ravel_multi_index(goal, SIZES))))
    return lax.ppermute(value, AXES, pairs)


def swap_core(value):
    return send(value, lambda x, z, y, k: (x, z, y, 1 - k))


def along_x(value, d):
    return send(value, lambda x, z, y, k: (x + d, z, y, k))


def along_y(value, d):
    return send(value, lambda x, z, y, k: (x, z, y + d, k))


def along_z(value, d):
    return send(value, lambda x, z, y, k: (x, z + d, y, k))


def first_leg(value, d):
    return send(value, lambda x, z, y, k: (x, z, y + d, k) if k == 0 else (x, z + d, y, k))


def second_leg(value, d):
    return send(value, lambda x, z, y, k: (x, z + d, y, k) if k == 0 else (x, z, y + d, k))


def gather4(value, move, index):
    out = jnp.zeros((4,) + value.shape, value.dtype)
    out = lax.dynamic_update_index_in_dim(out, value, index, 0)
    for d in (1, 2, 3):
        out = lax.dynamic_update_index_in_dim(out, move(value, d), (index - d) % 4, 0)
    return out


def gather_back(value, move):
    return jnp.stack([value] + [move(value, d) for d in (1, 2, 3)])


def softmax_rows(scores, valid):
    masked = jnp.where(valid, scores, neg_fill)
    top = jnp.max(masked, axis=-1, keepdims=True)
    expo = jnp.exp(masked - top)
    return expo / jnp.sum(expo, axis=-1, keepdims=True)


def dot(a, b):
    return jnp.dot(a, b, preferred_element_type=f32)


def rms_scale(values, gain):
    mean_sq = jnp.mean(values * values, axis=-1, keepdims=True)
    return values * lax.rsqrt(mean_sq + eps) * gain


def fine_normed(rows, gain):
    return rms_scale(rows.astype(f32), gain).astype(bf16)


def fine_attention(position, queries, keys, values):
    span = queries.shape[0]
    queries = queries.reshape(span, FH, 128)
    keys = keys.reshape(2 * span, FH, 128)
    values = values.reshape(2 * span, FH, 128)
    scores = jnp.einsum("qhd,khd->hqk", queries, keys, preferred_element_type=f32) * 128 ** (-0.5)
    query_index = jnp.arange(span, dtype=jnp.int32)[:, None]
    key_index = jnp.arange(2 * span, dtype=jnp.int32)[None, :]
    valid = (
        (key_index > query_index)
        & (key_index <= query_index + span)
        & (key_index + position * span >= span)
    )
    weights = softmax_rows(scores, valid[None]).astype(bf16)
    mixed = jnp.einsum("hqk,khd->qhd", weights, values, preferred_element_type=f32)
    return mixed.astype(bf16).reshape(span, DF)


def fold(up, gain, weight):
    rows = []
    for row in range(2):
        blocks = [up[2 * row + k, y, :384] for y in range(4) for k in range(2)]
        rows.append(jnp.concatenate(blocks, axis=1))
    block = (jnp.concatenate(rows, axis=0).astype(f32) * gain).astype(bf16)
    return dot(block, weight).astype(bf16)


def body(
    byte_in,
    flags,
    fine_gain,
    fine_qkv,
    fine_out,
    up_weight,
    coarse_gain,
    q_weight,
    kv_weight,
    out_weight,
):
    x, z, y, core = (lax.axis_index(name) for name in AXES)
    position = z * 8 + y * 2 + core
    first_index = jnp.where(core == 0, y, z)
    second_index = jnp.where(core == 0, z, y)
    columns = 32
    stretches = CPD * columns
    half = stretches // 2
    embedded = byte_in[0]
    four = jnp.arange(4, dtype=jnp.int32)

    def following(x, z, y, k):
        c = (z * 8 + y * 2 + k + 1) % 32
        return (x, c // 8, c // 2 % 4, c % 2)

    earlier = send(embedded, following)

    def turn(x, z, y, k):
        second = 2 * (x % 2) + k
        return (z, second, y, 0) if x < 2 else (z, y, second, 1)

    turned = send(up_weight, turn)

    out_turned = send(out_weight, lambda x, z, y, k: (2 * x - z, x, y, k))
    qkv = jnp.transpose(fine_qkv, (1, 0, 2))
    normed = fine_normed(embedded, fine_gain)
    normed, flags = lax.optimization_barrier((normed, flags))

    flag_row = flags[0]
    local = jnp.cumsum(flag_row) - 1
    count = jnp.sum(flag_row)
    head_len = jnp.sum((local < 0).astype(jnp.int32))
    last_len = jnp.sum((local == count - 1).astype(jnp.int32))
    lane = jnp.arange(256, dtype=jnp.int32)[None, :]
    facts = jnp.where(lane == 0, count, jnp.where(lane == 1, head_len, last_len)).astype(bf16)
    facts = jnp.broadcast_to(facts, (16, 256))
    queries = dot(normed, qkv[0]).astype(bf16)
    turned, queries, earlier, q_weight, kv_weight = lax.optimization_barrier(
        (turned, queries, earlier, q_weight, kv_weight)
    )

    payload = jnp.concatenate([turned, facts], axis=0)
    up_row = gather4(payload, first_leg, first_index)
    kv_turned = jnp.transpose(kv_weight, (1, 2, 0)).reshape(64, 2048)
    q_other = swap_core(q_weight)
    kv_far_core = swap_core(kv_turned)
    both = jnp.concatenate([fine_normed(earlier, fine_gain), normed], axis=0)
    keys = dot(both, qkv[1]).astype(bf16)
    values = dot(both, qkv[2]).astype(bf16)
    up_row, keys, values, out_turned, q_other, kv_far_core = lax.optimization_barrier(
        (up_row, keys, values, out_turned, q_other, kv_far_core)
    )

    over_x = lax.all_gather(jnp.concatenate([out_turned, up_weight], axis=0), "x", axis=0)
    kv_both = jnp.concatenate([kv_turned, kv_far_core], axis=0).T
    qkv_weight = jnp.concatenate([q_weight, q_other, kv_both], axis=1)
    up_block = gather4(up_row, second_leg, second_index)
    mixed = fine_attention(position, queries, keys, values)
    hidden = (embedded.astype(f32) + dot(mixed, fine_out)).astype(bf16)

    slot_index = jnp.arange(SLOTS, dtype=jnp.int32)
    slot_of = jnp.where(local < 0, MAXC, local)
    slot_table = slot_of[None, :] == slot_index[:, None]
    lens = jnp.sum(slot_table.astype(jnp.int32), axis=1)
    as_sum = (slot_index == MAXC) | (slot_index == count - 1)
    inverse = jnp.where(as_sum, 1.0, 1.0 / jnp.maximum(lens, 1).astype(f32)).reshape(SLOTS, 1)
    slots = (dot(slot_table.astype(bf16), hidden) * inverse).astype(bf16)
    slots = jnp.stack([slots[:, :768], slots[:, 768:]])
    mine = lax.dynamic_index_in_dim(slots, core, 0, keepdims=False)
    other = lax.dynamic_index_in_dim(slots, 1 - core, 0, keepdims=False)
    pair = jnp.stack([mine, swap_core(other)])
    pair, up_block, qkv_weight = lax.optimization_barrier((pair, up_block, qkv_weight))
    slots_row = gather_back(pair, first_leg)

    facts = up_block[:, :, 384, :128].astype(f32)
    facts = jnp.where(core == 0, facts, jnp.swapaxes(facts, 0, 1)).reshape(16, 128)
    facts_other = swap_core(facts)
    facts = jnp.where(
        core == 0, jnp.stack([facts, facts_other], axis=1), jnp.stack([facts_other, facts], axis=1)
    )
    facts = facts.reshape(columns, 128).astype(jnp.int32)
    counts = facts[:, 0]
    begins = jnp.cumsum(counts) - counts
    whole_last = facts[:, 2] + jnp.concatenate([facts[1:, 1], jnp.zeros((1,), jnp.int32)])

    gain_block = lax.dynamic_slice_in_dim(coarse_gain, x * 2048, 2048, 0)
    folded = fold(up_block, gain_block, qkv_weight).reshape(4, 192, 640)
    folded, slots_row = lax.optimization_barrier((folded, slots_row))
    total = lax.dynamic_index_in_dim(folded, x, 0, keepdims=False).astype(f32)
    all_slots = gather_back(slots_row, second_leg)
    for d in (1, 2, 3):
        piece = lax.dynamic_index_in_dim(folded, (x + d) % 4, 0, keepdims=False)
        total = total + along_x(piece, d).astype(f32)
    folded = gather4(total.astype(bf16), along_x, x).reshape(768, 640)
    arrived = swap_core(folded[:, 256:])
    q_cols = jnp.stack([folded[:, :256], arrived[:, :256]])
    kv_mine = jnp.stack([folded[:, 512:576], arrived[:, 320:]])
    kv_other = jnp.stack([folded[:, 576:], arrived[:, 256:320]])
    kv_near = jnp.where(
        core == 0,
        jnp.concatenate([kv_mine, kv_other], axis=2),
        jnp.concatenate([kv_other, kv_mine], axis=2),
    )
    kv_far = send(kv_near, lambda x, z, y, k: (x, z, y ^ 1, k))
    all_slots = all_slots.reshape(columns * SLOTS, 768)

    first_of = (first_index - four[None, :, None]) % 4
    second_of = (second_index - four[:, None, None]) % 4
    core_of = jnp.array([0, 1], jnp.int32)[None, None, :] ^ core
    device_of = jnp.where(core == 0, second_of * 8 + first_of * 2, first_of * 8 + second_of * 2)
    device_of = (device_of + core_of).reshape(columns, 1)
    is_device = device_of == jnp.arange(columns, dtype=jnp.int32)[None, :]
    begin_of = jnp.sum(jnp.where(is_device, begins[None, :], 0), axis=1, keepdims=True)
    count_of = jnp.sum(jnp.where(is_device, counts[None, :], 0), axis=1, keepdims=True)
    place = jnp.where(
        slot_index[None, :] == MAXC,
        begin_of - 1,
        jnp.where(slot_index[None, :] < count_of, begin_of + slot_index[None, :], -1),
    ).reshape(1, columns * SLOTS)
    choose = (place == jnp.arange(stretches, dtype=jnp.int32)[:, None]).astype(bf16)
    row = jnp.arange(stretches, dtype=jnp.int32)[:, None]
    is_last = row == (begins + counts - 1)[None, :]
    row_len = jnp.sum(jnp.where(is_last, whole_last[None, :], 0), axis=1, keepdims=True)
    row_scale = 1.0 / jnp.maximum(row_len, 1).astype(f32)
    pooled = (dot(choose, all_slots) * row_scale).astype(bf16)
    pooled_other = swap_core(pooled)
    pooled_other, over_x = lax.optimization_barrier((pooled_other, over_x))
    out_mine = over_x[:, :2048]
    up_cols = over_x[:, 2048:].reshape(2, 768, 256)
    up_cols = jnp.where(core == 0, up_cols, up_cols[::-1])

    out_other = swap_core(out_mine)
    out_rows = []
    for d in range(4):
        pieces = []
        for e in range(4):
            at = ((z - e) % 4, (y - d) % 4 * 512, 0)
            own = lax.dynamic_slice(out_mine, at, (1, 512, 256))[0]
            far = lax.dynamic_slice(out_other, at, (1, 512, 256))[0]
            pieces += [own, far]
        out_rows.append(jnp.concatenate(pieces, axis=1))
    out_block = jnp.concatenate(out_rows, axis=0)


    up_out = dot(pooled, up_cols[0]) + dot(pooled_other, up_cols[1])
    coarse_in = up_out.astype(bf16)
    coarse_f32 = coarse_in.astype(f32)
    squares = jnp.sum(coarse_f32 * coarse_f32, axis=1).reshape(1, stretches)
    squares = squares + swap_core(squares)
    squares, kv_far = lax.optimization_barrier((squares, kv_far))
    kv_all = jnp.where(
        y % 2 == 0,
        jnp.concatenate([kv_near, kv_far], axis=2),
        jnp.concatenate([kv_far, kv_near], axis=2),
    )
    kv_all = kv_all.reshape(2, 768, 4, 2, 32).transpose(0, 1, 3, 2, 4).reshape(2, 768, 256)
    weights_all = jnp.concatenate([q_cols, kv_all], axis=2)
    squares = squares + sum(along_y(squares, d) for d in (1, 2, 3))
    squares = squares + sum(along_z(squares, d) for d in (1, 2, 3))
    scale = lax.rsqrt(squares / DC + eps).reshape(stretches, 1)
    qkv = dot(pooled, weights_all[0]) + dot(pooled_other, weights_all[1])
    qkv = (qkv * scale).astype(bf16)
    head = DC // HEADS
    queries = qkv[:, :256].reshape(stretches, 2, head)
    keys = qkv[:, 256 : 256 + head]
    values = qkv[:, 256 + head :]
    scores = jnp.einsum("qhd,kd->hqk", queries, keys, preferred_element_type=f32) * head ** (-0.5)
    rows = jnp.arange(stretches, dtype=jnp.int32)
    causal = rows[:, None] >= rows[None, :]
    coarse_weights = softmax_rows(scores, causal).astype(bf16)
    mix = jnp.einsum("hqk,kd->qhd", coarse_weights, values, preferred_element_type=f32)
    mix = mix.astype(bf16).reshape(2, half, 256)

    mine = lax.dynamic_index_in_dim(mix, core, 0, keepdims=False)
    other = lax.dynamic_index_in_dim(mix, 1 - core, 0, keepdims=False)
    got = swap_core(other)
    pair = jnp.where(
        core == 0, jnp.concatenate([mine, got], axis=1), jnp.concatenate([got, mine], axis=1)
    )
    branches = []
    for part in (pair[: half // 2], pair[half // 2 :]):
        group = jnp.concatenate([part] + [along_y(part, d) for d in (1, 2, 3)], axis=1)
        partial = dot(group, out_block)
        branch = partial[:, :512]
        for d in (1, 2, 3):
            piece = partial[:, d * 512 : (d + 1) * 512].astype(bf16)
            branch = branch + along_z(piece, d).astype(f32)
        branches.append(branch)
    branch = jnp.concatenate(branches, axis=0)
    branch_other = swap_core(branch[:, 256:].astype(bf16)).astype(f32)
    branch = jnp.where(
        core == 0,
        jnp.stack([branch[:, :256], branch_other]),
        jnp.stack([branch_other, branch[:, :256]]),
    ).reshape(stretches, 256)
    coarse_out = (coarse_f32 + branch).astype(bf16)
    return (hidden.reshape(1, 128, DF), coarse_out.reshape(1, stretches, 256))


def solution(mesh):
    grid = Mesh(mesh.devices.reshape(SIZES), AXES)
    col = ("z", "y", "core")
    in_specs = (
        P("x", col, None),
        P("x", col),
        P(),
        P(),
        P(),
        P("x", col),
        P(),
        P("x", col),
        P("x", None, col),
        P("x", col),
    )
    out_specs = (P("x", col, None), P("x", None, col))
    return jax.shard_map(body, mesh=grid, in_specs=in_specs, out_specs=out_specs, check_vma=False)
```

```python
import jax
import jax.numpy as jnp
import numpy as np
from jax import lax
from jax.sharding import Mesh, PartitionSpec as P

DF = 1536
FH = 12
DC = 8192
HEADS = 64
KVH = 8
CPD = 22
MAXC = 66
SLOTS = 72
AXES = ("x", "z", "y", "core")
SIZES = (4, 4, 4, 2)

eps = 1e-05
neg_fill = -1e30
bf16 = jnp.bfloat16
f32 = jnp.float32


def send(value, target):
    pairs = []
    for source in range(128):
        where = tuple(int(i) for i in np.unravel_index(source, SIZES))
        goal = tuple(int(i) % n for i, n in zip(target(*where), SIZES))
        pairs.append((source, int(np.ravel_multi_index(goal, SIZES))))
    return lax.ppermute(value, AXES, pairs)


def swap_core(value):
    return send(value, lambda x, z, y, k: (x, z, y, 1 - k))


def along_x(value, d):
    return send(value, lambda x, z, y, k: (x + d, z, y, k))


def along_y(value, d):
    return send(value, lambda x, z, y, k: (x, z, y + d, k))


def along_z(value, d):
    return send(value, lambda x, z, y, k: (x, z + d, y, k))


def first_leg(value, d):
    return send(value, lambda x, z, y, k: (x, z, y + d, k) if k == 0 else (x, z + d, y, k))


def second_leg(value, d):
    return send(value, lambda x, z, y, k: (x, z + d, y, k) if k == 0 else (x, z, y + d, k))


def gather4(value, move, index):
    out = jnp.zeros((4,) + value.shape, value.dtype)
    out = lax.dynamic_update_index_in_dim(out, value, index, 0)
    for d in (1, 2, 3):
        out = lax.dynamic_update_index_in_dim(out, move(value, d), (index - d) % 4, 0)
    return out


def gather_back(value, move):
    return jnp.stack([value] + [move(value, d) for d in (1, 2, 3)])


def softmax_rows(scores, valid):
    masked = jnp.where(valid, scores, neg_fill)
    top = jnp.max(masked, axis=-1, keepdims=True)
    expo = jnp.exp(masked - top)
    return expo / jnp.sum(expo, axis=-1, keepdims=True)


def dot(a, b):
    return jnp.dot(a, b, preferred_element_type=f32)


def rms_scale(values, gain):
    mean_sq = jnp.mean(values * values, axis=-1, keepdims=True)
    return values * lax.rsqrt(mean_sq + eps) * gain


def fine_normed(rows, gain):
    return rms_scale(rows.astype(f32), gain).astype(bf16)


def fine_attention(position, queries, keys, values):
    span = queries.shape[0]
    queries = queries.reshape(span, FH, 128)
    keys = keys.reshape(2 * span, FH, 128)
    values = values.reshape(2 * span, FH, 128)
    scores = jnp.einsum("qhd,khd->hqk", queries, keys, preferred_element_type=f32) * 128 ** (-0.5)
    query_index = jnp.arange(span, dtype=jnp.int32)[:, None]
    key_index = jnp.arange(2 * span, dtype=jnp.int32)[None, :]
    valid = (
        (key_index > query_index)
        & (key_index <= query_index + span)
        & (key_index + position * span >= span)
    )
    weights = softmax_rows(scores, valid[None]).astype(bf16)
    mixed = jnp.einsum("hqk,khd->qhd", weights, values, preferred_element_type=f32)
    return mixed.astype(bf16).reshape(span, DF)


def fold(up, gain, weight):
    rows = []
    for row in range(2):
        blocks = [up[2 * row + k, y, :384] for y in range(4) for k in range(2)]
        rows.append(jnp.concatenate(blocks, axis=1))
    block = (jnp.concatenate(rows, axis=0).astype(f32) * gain).astype(bf16)
    return dot(block, weight).astype(bf16)


def body(
    byte_in,
    flags,
    fine_gain,
    fine_qkv,
    fine_out,
    up_weight,
    coarse_gain,
    q_weight,
    kv_weight,
    out_weight,
):
    x, z, y, core = (lax.axis_index(name) for name in AXES)
    position = z * 8 + y * 2 + core
    first_index = jnp.where(core == 0, y, z)
    second_index = jnp.where(core == 0, z, y)
    columns = 32
    stretches = CPD * columns
    half = stretches // 2
    embedded = byte_in[0]
    four = jnp.arange(4, dtype=jnp.int32)

    def following(x, z, y, k):
        c = (z * 8 + y * 2 + k + 1) % 32
        return (x, c // 8, c // 2 % 4, c % 2)

    earlier = send(embedded, following)

    def turn(x, z, y, k):
        second = 2 * (x % 2) + k
        return (z, second, y, 0) if x < 2 else (z, y, second, 1)

    turned = send(up_weight, turn)

    out_turned = send(out_weight, lambda x, z, y, k: (2 * x - z, x, y, k))
    qkv = jnp.transpose(fine_qkv, (1, 0, 2))
    normed = fine_normed(embedded, fine_gain)
    normed, flags = lax.optimization_barrier((normed, flags))

    flag_row = flags[0]
    local = jnp.cumsum(flag_row) - 1
    count = jnp.sum(flag_row)
    head_len = jnp.sum((local < 0).astype(jnp.int32))
    last_len = jnp.sum((local == count - 1).astype(jnp.int32))
    lane = jnp.arange(256, dtype=jnp.int32)[None, :]
    facts = jnp.where(lane == 0, count, jnp.where(lane == 1, head_len, last_len)).astype(bf16)
    facts = jnp.broadcast_to(facts, (16, 256))
    queries = dot(normed, qkv[0]).astype(bf16)
    turned, queries, earlier, q_weight, kv_weight = lax.optimization_barrier(
        (turned, queries, earlier, q_weight, kv_weight)
    )

    payload = jnp.concatenate([turned, facts], axis=0)
    up_row = gather4(payload, first_leg, first_index)
    kv_turned = jnp.transpose(kv_weight, (1, 2, 0)).reshape(64, 2048)
    q_other = swap_core(q_weight)
    kv_far_core = swap_core(kv_turned)
    both = jnp.concatenate([fine_normed(earlier, fine_gain), normed], axis=0)
    keys = dot(both, qkv[1]).astype(bf16)
    values = dot(both, qkv[2]).astype(bf16)
    up_row, keys, values, out_turned, q_other, kv_far_core = lax.optimization_barrier(
        (up_row, keys, values, out_turned, q_other, kv_far_core)
    )

    over_x = lax.all_gather(jnp.concatenate([out_turned, up_weight], axis=0), "x", axis=0)
    kv_both = jnp.concatenate([kv_turned, kv_far_core], axis=0).T
    qkv_weight = jnp.concatenate([q_weight, q_other, kv_both], axis=1)
    up_block = gather4(up_row, second_leg, second_index)
    mixed = fine_attention(position, queries, keys, values)
    hidden = (embedded.astype(f32) + dot(mixed, fine_out)).astype(bf16)

    slot_index = jnp.arange(SLOTS, dtype=jnp.int32)
    slot_of = jnp.where(local < 0, MAXC, local)
    slot_table = slot_of[None, :] == slot_index[:, None]
    lens = jnp.sum(slot_table.astype(jnp.int32), axis=1)
    as_sum = (slot_index == MAXC) | (slot_index == count - 1)
    inverse = jnp.where(as_sum, 1.0, 1.0 / jnp.maximum(lens, 1).astype(f32)).reshape(SLOTS, 1)
    slots = (dot(slot_table.astype(bf16), hidden) * inverse).astype(bf16)
    slots = jnp.stack([slots[:, :768], slots[:, 768:]])
    mine = lax.dynamic_index_in_dim(slots, core, 0, keepdims=False)
    other = lax.dynamic_index_in_dim(slots, 1 - core, 0, keepdims=False)
    pair = jnp.stack([mine, swap_core(other)])
    pair, up_block, qkv_weight = lax.optimization_barrier((pair, up_block, qkv_weight))
    slots_row = gather_back(pair, first_leg)

    facts = up_block[:, :, 384, :128].astype(f32)
    facts = jnp.where(core == 0, facts, jnp.swapaxes(facts, 0, 1)).reshape(16, 128)
    facts_other = swap_core(facts)
    facts = jnp.where(
        core == 0, jnp.stack([facts, facts_other], axis=1), jnp.stack([facts_other, facts], axis=1)
    )
    facts = facts.reshape(columns, 128).astype(jnp.int32)
    counts = facts[:, 0]
    begins = jnp.cumsum(counts) - counts
    whole_last = facts[:, 2] + jnp.concatenate([facts[1:, 1], jnp.zeros((1,), jnp.int32)])

    gain_block = lax.dynamic_slice_in_dim(coarse_gain, x * 2048, 2048, 0)
    folded = fold(up_block, gain_block, qkv_weight).reshape(4, 192, 640)
    folded, slots_row = lax.optimization_barrier((folded, slots_row))
    total = lax.dynamic_index_in_dim(folded, x, 0, keepdims=False).astype(f32)
    all_slots = gather_back(slots_row, second_leg)
    for d in (1, 2, 3):
        piece = lax.dynamic_index_in_dim(folded, (x + d) % 4, 0, keepdims=False)
        total = total + along_x(piece, d).astype(f32)
    total, over_x = lax.optimization_barrier((total.astype(bf16), over_x))
    total_far = [along_x(total, d) for d in (1, 2, 3)]

    all_slots = all_slots.reshape(columns * SLOTS, 768)

    first_of = (first_index - four[None, :, None]) % 4
    second_of = (second_index - four[:, None, None]) % 4
    core_of = jnp.array([0, 1], jnp.int32)[None, None, :] ^ core
    device_of = jnp.where(core == 0, second_of * 8 + first_of * 2, first_of * 8 + second_of * 2)
    device_of = (device_of + core_of).reshape(columns, 1)
    is_device = device_of == jnp.arange(columns, dtype=jnp.int32)[None, :]
    begin_of = jnp.sum(jnp.where(is_device, begins[None, :], 0), axis=1, keepdims=True)
    count_of = jnp.sum(jnp.where(is_device, counts[None, :], 0), axis=1, keepdims=True)
    place = jnp.where(
        slot_index[None, :] == MAXC,
        begin_of - 1,
        jnp.where(slot_index[None, :] < count_of, begin_of + slot_index[None, :], -1),
    ).reshape(1, columns * SLOTS)
    choose = (place == jnp.arange(stretches, dtype=jnp.int32)[:, None]).astype(bf16)
    row = jnp.arange(stretches, dtype=jnp.int32)[:, None]
    is_last = row == (begins + counts - 1)[None, :]
    row_len = jnp.sum(jnp.where(is_last, whole_last[None, :], 0), axis=1, keepdims=True)
    row_scale = 1.0 / jnp.maximum(row_len, 1).astype(f32)
    pooled = (dot(choose, all_slots) * row_scale).astype(bf16)
    pooled, *total_far = lax.optimization_barrier((pooled, *total_far))
    folded = lax.dynamic_update_index_in_dim(jnp.zeros((4, 192, 640), bf16), total, x, 0)
    for d, block in enumerate(total_far, 1):
        folded = lax.dynamic_update_index_in_dim(folded, block, (x - d) % 4, 0)
    folded = folded.reshape(768, 640)
    arrived = swap_core(folded[:, 256:])
    q_cols = jnp.stack([folded[:, :256], arrived[:, :256]])
    kv_mine = jnp.stack([folded[:, 512:576], arrived[:, 320:]])
    kv_other = jnp.stack([folded[:, 576:], arrived[:, 256:320]])
    kv_near = jnp.where(
        core == 0,
        jnp.concatenate([kv_mine, kv_other], axis=2),
        jnp.concatenate([kv_other, kv_mine], axis=2),
    )
    kv_far = send(kv_near, lambda x, z, y, k: (x, z, y ^ 1, k))
    pooled_other = swap_core(pooled)
    pooled_other, out_mine = lax.optimization_barrier((pooled_other, over_x))
    up_cols = out_mine[:, 2048:].reshape(2, 768, 256)
    up_cols = jnp.where(core == 0, up_cols, up_cols[::-1])

    out_other = swap_core(out_mine)
    out_rows = []
    for d in range(4):
        pieces = []
        for e in range(4):
            at = ((z - e) % 4, (y - d) % 4 * 512, 0)
            own = lax.dynamic_slice(out_mine, at, (1, 512, 256))[0]
            far = lax.dynamic_slice(out_other, at, (1, 512, 256))[0]
            pieces += [own, far]
        out_rows.append(jnp.concatenate(pieces, axis=1))
    out_block = jnp.concatenate(out_rows, axis=0)


    up_out = dot(pooled, up_cols[0]) + dot(pooled_other, up_cols[1])
    coarse_in = up_out.astype(bf16)
    coarse_f32 = coarse_in.astype(f32)
    squares = jnp.sum(coarse_f32 * coarse_f32, axis=1).reshape(1, stretches)
    squares = squares + swap_core(squares)
    squares, kv_far = lax.optimization_barrier((squares, kv_far))
    kv_all = jnp.where(
        y % 2 == 0,
        jnp.concatenate([kv_near, kv_far], axis=2),
        jnp.concatenate([kv_far, kv_near], axis=2),
    )
    kv_all = kv_all.reshape(2, 768, 4, 2, 32).transpose(0, 1, 3, 2, 4).reshape(2, 768, 256)
    weights_all = jnp.concatenate([q_cols, kv_all], axis=2)
    squares = squares + sum(along_y(squares, d) for d in (1, 2, 3))
    squares = squares + sum(along_z(squares, d) for d in (1, 2, 3))
    scale = lax.rsqrt(squares / DC + eps).reshape(stretches, 1)
    qkv = dot(pooled, weights_all[0]) + dot(pooled_other, weights_all[1])
    qkv = (qkv * scale).astype(bf16)
    head = DC // HEADS
    queries = qkv[:, :256].reshape(stretches, 2, head)
    keys = qkv[:, 256 : 256 + head]
    values = qkv[:, 256 + head :]
    scores = jnp.einsum("qhd,kd->hqk", queries, keys, preferred_element_type=f32) * head ** (-0.5)
    rows = jnp.arange(stretches, dtype=jnp.int32)
    causal = rows[:, None] >= rows[None, :]
    coarse_weights = softmax_rows(scores, causal).astype(bf16)
    mix = jnp.einsum("hqk,kd->qhd", coarse_weights, values, preferred_element_type=f32)
    mix = mix.astype(bf16).reshape(2, half, 256)

    mine = lax.dynamic_index_in_dim(mix, core, 0, keepdims=False)
    other = lax.dynamic_index_in_dim(mix, 1 - core, 0, keepdims=False)
    got = swap_core(other)
    pair = jnp.where(
        core == 0, jnp.concatenate([mine, got], axis=1), jnp.concatenate([got, mine], axis=1)
    )
    branches = []
    for part in (pair[: half // 2], pair[half // 2 :]):
        group = jnp.concatenate([part] + [along_y(part, d) for d in (1, 2, 3)], axis=1)
        partial = dot(group, out_block)
        branch = partial[:, :512]
        for d in (1, 2, 3):
            piece = partial[:, d * 512 : (d + 1) * 512].astype(bf16)
            branch = branch + along_z(piece, d).astype(f32)
        branches.append(branch)
    branch = jnp.concatenate(branches, axis=0)
    branch_other = swap_core(branch[:, 256:].astype(bf16)).astype(f32)
    branch = jnp.where(
        core == 0,
        jnp.stack([branch[:, :256], branch_other]),
        jnp.stack([branch_other, branch[:, :256]]),
    ).reshape(stretches, 256)
    coarse_out = (coarse_f32 + branch).astype(bf16)
    return (hidden.reshape(1, 128, DF), coarse_out.reshape(1, stretches, 256))


def solution(mesh):
    grid = Mesh(mesh.devices.reshape(SIZES), AXES)
    col = ("z", "y", "core")
    in_specs = (
        P("x", col, None),
        P("x", col),
        P(),
        P(),
        P(),
        P("x", col),
        P(),
        P("x", col),
        P("x", None, col),
        P("x", col),
    )
    out_specs = (P("x", col, None), P("x", None, col))
    return jax.shard_map(body, mesh=grid, in_specs=in_specs, out_specs=out_specs, check_vma=False)
```

```python
import jax
import jax.numpy as jnp
import numpy as np
from jax import lax
from jax.sharding import Mesh, PartitionSpec as P

DF = 1536
FH = 12
DC = 8192
HEADS = 64
KVH = 8
CPD = 22
MAXC = 66
SLOTS = 72
AXES = ("x", "z", "y", "core")
SIZES = (4, 4, 4, 2)

eps = 1e-05
neg_fill = -1e30
bf16 = jnp.bfloat16
f32 = jnp.float32


def send(value, target):
    pairs = []
    for source in range(128):
        where = tuple(int(i) for i in np.unravel_index(source, SIZES))
        goal = tuple(int(i) % n for i, n in zip(target(*where), SIZES))
        pairs.append((source, int(np.ravel_multi_index(goal, SIZES))))
    return lax.ppermute(value, AXES, pairs)


def swap_core(value):
    return send(value, lambda x, z, y, k: (x, z, y, 1 - k))


def along_x(value, d):
    return send(value, lambda x, z, y, k: (x + d, z, y, k))


def along_y(value, d):
    return send(value, lambda x, z, y, k: (x, z, y + d, k))


def along_z(value, d):
    return send(value, lambda x, z, y, k: (x, z + d, y, k))


def first_leg(value, d):
    return send(value, lambda x, z, y, k: (x, z, y + d, k) if k == 0 else (x, z + d, y, k))


def second_leg(value, d):
    return send(value, lambda x, z, y, k: (x, z + d, y, k) if k == 0 else (x, z, y + d, k))


def gather4(value, move, index):
    out = jnp.zeros((4,) + value.shape, value.dtype)
    out = lax.dynamic_update_index_in_dim(out, value, index, 0)
    for d in (1, 2, 3):
        out = lax.dynamic_update_index_in_dim(out, move(value, d), (index - d) % 4, 0)
    return out


def gather_back(value, move):
    return jnp.stack([value] + [move(value, d) for d in (1, 2, 3)])


def softmax_rows(scores, valid):
    masked = jnp.where(valid, scores, neg_fill)
    top = jnp.max(masked, axis=-1, keepdims=True)
    expo = jnp.exp(masked - top)
    return expo / jnp.sum(expo, axis=-1, keepdims=True)


def dot(a, b):
    return jnp.dot(a, b, preferred_element_type=f32)


def rms_scale(values, gain):
    mean_sq = jnp.mean(values * values, axis=-1, keepdims=True)
    return values * lax.rsqrt(mean_sq + eps) * gain


def fine_normed(rows, gain):
    return rms_scale(rows.astype(f32), gain).astype(bf16)


def fine_attention(position, queries, keys, values):
    span = queries.shape[0]
    queries = queries.reshape(span, FH, 128)
    keys = keys.reshape(2 * span, FH, 128)
    values = values.reshape(2 * span, FH, 128)
    scores = jnp.einsum("qhd,khd->hqk", queries, keys, preferred_element_type=f32) * 128 ** (-0.5)
    query_index = jnp.arange(span, dtype=jnp.int32)[:, None]
    key_index = jnp.arange(2 * span, dtype=jnp.int32)[None, :]
    valid = (
        (key_index > query_index)
        & (key_index <= query_index + span)
        & (key_index + position * span >= span)
    )
    weights = softmax_rows(scores, valid[None]).astype(bf16)
    mixed = jnp.einsum("hqk,khd->qhd", weights, values, preferred_element_type=f32)
    return mixed.astype(bf16).reshape(span, DF)


def fold(up, gain, weight):
    rows = []
    for row in range(2):
        blocks = [up[2 * row + k, y, :384] for y in range(4) for k in range(2)]
        rows.append(jnp.concatenate(blocks, axis=1))
    block = (jnp.concatenate(rows, axis=0).astype(f32) * gain).astype(bf16)
    return dot(block, weight).astype(bf16)


def body(
    byte_in,
    flags,
    fine_gain,
    fine_qkv,
    fine_out,
    up_weight,
    coarse_gain,
    q_weight,
    kv_weight,
    out_weight,
):
    x, z, y, core = (lax.axis_index(name) for name in AXES)
    position = z * 8 + y * 2 + core
    first_index = jnp.where(core == 0, y, z)
    second_index = jnp.where(core == 0, z, y)
    columns = 32
    stretches = CPD * columns
    half = stretches // 2
    embedded = byte_in[0]
    four = jnp.arange(4, dtype=jnp.int32)

    def following(x, z, y, k):
        c = (z * 8 + y * 2 + k + 1) % 32
        return (x, c // 8, c // 2 % 4, c % 2)

    earlier = send(embedded, following)

    def turn(x, z, y, k):
        second = 2 * (x % 2) + k
        return (z, second, y, 0) if x < 2 else (z, y, second, 1)

    turned = send(up_weight, turn)

    qkv = jnp.transpose(fine_qkv, (1, 0, 2))
    normed = fine_normed(embedded, fine_gain)
    normed, flags = lax.optimization_barrier((normed, flags))

    flag_row = flags[0]
    local = jnp.cumsum(flag_row) - 1
    count = jnp.sum(flag_row)
    head_len = jnp.sum((local < 0).astype(jnp.int32))
    last_len = jnp.sum((local == count - 1).astype(jnp.int32))
    lane = jnp.arange(256, dtype=jnp.int32)[None, :]
    facts = jnp.where(lane == 0, count, jnp.where(lane == 1, head_len, last_len)).astype(bf16)
    facts = jnp.broadcast_to(facts, (16, 256))
    queries = dot(normed, qkv[0]).astype(bf16)
    turned, queries, earlier, q_weight, kv_weight = lax.optimization_barrier(
        (turned, queries, earlier, q_weight, kv_weight)
    )

    payload = jnp.concatenate([turned, facts], axis=0)
    up_row = gather4(payload, first_leg, first_index)
    kv_turned = jnp.transpose(kv_weight, (1, 2, 0)).reshape(64, 2048)
    q_other = swap_core(q_weight)
    kv_far_core = swap_core(kv_turned)
    both = jnp.concatenate([fine_normed(earlier, fine_gain), normed], axis=0)
    keys = dot(both, qkv[1]).astype(bf16)
    values = dot(both, qkv[2]).astype(bf16)
    up_row, keys, values, out_weight, q_other, kv_far_core = lax.optimization_barrier(
        (up_row, keys, values, out_weight, q_other, kv_far_core)
    )
    out_turned = send(out_weight, lambda x, z, y, k: (2 * x - z, x, y, k))

    kv_both = jnp.concatenate([kv_turned, kv_far_core], axis=0).T
    qkv_weight = jnp.concatenate([q_weight, q_other, kv_both], axis=1)
    up_block = gather4(up_row, second_leg, second_index)
    mixed = fine_attention(position, queries, keys, values)
    hidden = (embedded.astype(f32) + dot(mixed, fine_out)).astype(bf16)

    slot_index = jnp.arange(SLOTS, dtype=jnp.int32)
    slot_of = jnp.where(local < 0, MAXC, local)
    slot_table = slot_of[None, :] == slot_index[:, None]
    lens = jnp.sum(slot_table.astype(jnp.int32), axis=1)
    as_sum = (slot_index == MAXC) | (slot_index == count - 1)
    inverse = jnp.where(as_sum, 1.0, 1.0 / jnp.maximum(lens, 1).astype(f32)).reshape(SLOTS, 1)
    slots = (dot(slot_table.astype(bf16), hidden) * inverse).astype(bf16)
    slots = jnp.stack([slots[:, :768], slots[:, 768:]])
    mine = lax.dynamic_index_in_dim(slots, core, 0, keepdims=False)
    other = lax.dynamic_index_in_dim(slots, 1 - core, 0, keepdims=False)
    pair = jnp.stack([mine, swap_core(other)])
    pair, up_block, qkv_weight, up_weight = lax.optimization_barrier(
        (pair, up_block, qkv_weight, up_weight)
    )
    up_cols = gather4(up_weight, along_x, x)
    slots_row = gather_back(pair, first_leg)

    facts = up_block[:, :, 384, :128].astype(f32)
    facts = jnp.where(core == 0, facts, jnp.swapaxes(facts, 0, 1)).reshape(16, 128)
    facts_other = swap_core(facts)
    facts = jnp.where(
        core == 0, jnp.stack([facts, facts_other], axis=1), jnp.stack([facts_other, facts], axis=1)
    )
    facts = facts.reshape(columns, 128).astype(jnp.int32)
    counts = facts[:, 0]
    begins = jnp.cumsum(counts) - counts
    whole_last = facts[:, 2] + jnp.concatenate([facts[1:, 1], jnp.zeros((1,), jnp.int32)])

    gain_block = lax.dynamic_slice_in_dim(coarse_gain, x * 2048, 2048, 0)
    folded = fold(up_block, gain_block, qkv_weight).reshape(4, 192, 640)
    folded, slots_row, up_cols, out_turned = lax.optimization_barrier(
        (folded, slots_row, up_cols, out_turned)
    )
    up_cols = up_cols.reshape(2, 768, 256)
    up_cols = jnp.where(core == 0, up_cols, up_cols[::-1])
    total = lax.dynamic_index_in_dim(folded, x, 0, keepdims=False).astype(f32)
    all_slots = gather_back(slots_row, second_leg)
    for d in (1, 2, 3):
        piece = lax.dynamic_index_in_dim(folded, (x + d) % 4, 0, keepdims=False)
        total = total + along_x(piece, d).astype(f32)
    total = total.astype(bf16)
    total_far = [along_x(total, d) for d in (1, 2, 3)]

    all_slots = all_slots.reshape(columns * SLOTS, 768)

    first_of = (first_index - four[None, :, None]) % 4
    second_of = (second_index - four[:, None, None]) % 4
    core_of = jnp.array([0, 1], jnp.int32)[None, None, :] ^ core
    device_of = jnp.where(core == 0, second_of * 8 + first_of * 2, first_of * 8 + second_of * 2)
    device_of = (device_of + core_of).reshape(columns, 1)
    is_device = device_of == jnp.arange(columns, dtype=jnp.int32)[None, :]
    begin_of = jnp.sum(jnp.where(is_device, begins[None, :], 0), axis=1, keepdims=True)
    count_of = jnp.sum(jnp.where(is_device, counts[None, :], 0), axis=1, keepdims=True)
    place = jnp.where(
        slot_index[None, :] == MAXC,
        begin_of - 1,
        jnp.where(slot_index[None, :] < count_of, begin_of + slot_index[None, :], -1),
    ).reshape(1, columns * SLOTS)
    choose = (place == jnp.arange(stretches, dtype=jnp.int32)[:, None]).astype(bf16)
    row = jnp.arange(stretches, dtype=jnp.int32)[:, None]
    is_last = row == (begins + counts - 1)[None, :]
    row_len = jnp.sum(jnp.where(is_last, whole_last[None, :], 0), axis=1, keepdims=True)
    row_scale = 1.0 / jnp.maximum(row_len, 1).astype(f32)
    pooled = (dot(choose, all_slots) * row_scale).astype(bf16)
    pooled, out_turned, *total_far = lax.optimization_barrier((pooled, out_turned, *total_far))
    over_x = lax.all_gather(out_turned, "x", axis=0)
    folded = lax.dynamic_update_index_in_dim(jnp.zeros((4, 192, 640), bf16), total, x, 0)
    for d, block in enumerate(total_far, 1):
        folded = lax.dynamic_update_index_in_dim(folded, block, (x - d) % 4, 0)
    folded = folded.reshape(768, 640)
    arrived = swap_core(folded[:, 256:])
    q_cols = jnp.stack([folded[:, :256], arrived[:, :256]])
    kv_mine = jnp.stack([folded[:, 512:576], arrived[:, 320:]])
    kv_other = jnp.stack([folded[:, 576:], arrived[:, 256:320]])
    kv_near = jnp.where(
        core == 0,
        jnp.concatenate([kv_mine, kv_other], axis=2),
        jnp.concatenate([kv_other, kv_mine], axis=2),
    )
    kv_far = send(kv_near, lambda x, z, y, k: (x, z, y ^ 1, k))
    pooled_other = swap_core(pooled)
    up_out = dot(pooled, up_cols[0]) + dot(pooled_other, up_cols[1])
    coarse_in = up_out.astype(bf16)
    coarse_f32 = coarse_in.astype(f32)
    squares = jnp.sum(coarse_f32 * coarse_f32, axis=1).reshape(1, stretches)
    squares = squares + swap_core(squares)
    squares, kv_far = lax.optimization_barrier((squares, kv_far))
    kv_all = jnp.where(
        y % 2 == 0,
        jnp.concatenate([kv_near, kv_far], axis=2),
        jnp.concatenate([kv_far, kv_near], axis=2),
    )
    kv_all = kv_all.reshape(2, 768, 4, 2, 32).transpose(0, 1, 3, 2, 4).reshape(2, 768, 256)
    weights_all = jnp.concatenate([q_cols, kv_all], axis=2)
    squares = squares + sum(along_y(squares, d) for d in (1, 2, 3))
    squares = squares + sum(along_z(squares, d) for d in (1, 2, 3))
    scale = lax.rsqrt(squares / DC + eps).reshape(stretches, 1)
    qkv = dot(pooled, weights_all[0]) + dot(pooled_other, weights_all[1])
    qkv = (qkv * scale).astype(bf16)
    head = DC // HEADS
    queries = qkv[:, :256].reshape(stretches, 2, head)
    keys = qkv[:, 256 : 256 + head]
    values = qkv[:, 256 + head :]
    scores = jnp.einsum("qhd,kd->hqk", queries, keys, preferred_element_type=f32) * head ** (-0.5)
    rows = jnp.arange(stretches, dtype=jnp.int32)
    causal = rows[:, None] >= rows[None, :]
    coarse_weights = softmax_rows(scores, causal).astype(bf16)
    mix = jnp.einsum("hqk,kd->qhd", coarse_weights, values, preferred_element_type=f32)
    mix = mix.astype(bf16).reshape(2, half, 256)
    mix, over_x = lax.optimization_barrier((mix, over_x))

    mine = lax.dynamic_index_in_dim(mix, core, 0, keepdims=False)
    other = lax.dynamic_index_in_dim(mix, 1 - core, 0, keepdims=False)
    got = swap_core(other)
    out_mine = over_x
    out_other = swap_core(out_mine)
    out_rows = []
    for d in range(4):
        pieces = []
        for e in range(4):
            at = ((z - e) % 4, (y - d) % 4 * 512, 0)
            own = lax.dynamic_slice(out_mine, at, (1, 512, 256))[0]
            far = lax.dynamic_slice(out_other, at, (1, 512, 256))[0]
            pieces += [own, far]
        out_rows.append(jnp.concatenate(pieces, axis=1))
    out_block = jnp.concatenate(out_rows, axis=0)
    pair = jnp.where(
        core == 0, jnp.concatenate([mine, got], axis=1), jnp.concatenate([got, mine], axis=1)
    )
    branches = []
    for part in (pair[: half // 2], pair[half // 2 :]):
        group = jnp.concatenate([part] + [along_y(part, d) for d in (1, 2, 3)], axis=1)
        partial = dot(group, out_block)
        branch = partial[:, :512]
        for d in (1, 2, 3):
            piece = partial[:, d * 512 : (d + 1) * 512].astype(bf16)
            branch = branch + along_z(piece, d).astype(f32)
        branches.append(branch)
    branch = jnp.concatenate(branches, axis=0)
    branch_other = swap_core(branch[:, 256:].astype(bf16)).astype(f32)
    branch = jnp.where(
        core == 0,
        jnp.stack([branch[:, :256], branch_other]),
        jnp.stack([branch_other, branch[:, :256]]),
    ).reshape(stretches, 256)
    coarse_out = (coarse_f32 + branch).astype(bf16)
    return (hidden.reshape(1, 128, DF), coarse_out.reshape(1, stretches, 256))


def solution(mesh):
    grid = Mesh(mesh.devices.reshape(SIZES), AXES)
    col = ("z", "y", "core")
    in_specs = (
        P("x", col, None),
        P("x", col),
        P(),
        P(),
        P(),
        P("x", col),
        P(),
        P("x", col),
        P("x", None, col),
        P("x", col),
    )
    out_specs = (P("x", col, None), P("x", None, col))
    return jax.shard_map(body, mesh=grid, in_specs=in_specs, out_specs=out_specs, check_vma=False)
```

```python
import jax
import jax.numpy as jnp
import numpy as np
from jax import lax
from jax.sharding import Mesh, PartitionSpec as P

DF = 1536
FH = 12
DC = 8192
HEADS = 64
KVH = 8
CPD = 22
MAXC = 66
SLOTS = 72
AXES = ("x", "z", "y", "core")
SIZES = (4, 4, 4, 2)

eps = 1e-05
neg_fill = -1e30
bf16 = jnp.bfloat16
f32 = jnp.float32


def send(value, target):
    pairs = []
    for source in range(128):
        where = tuple(int(i) for i in np.unravel_index(source, SIZES))
        goal = tuple(int(i) % n for i, n in zip(target(*where), SIZES))
        pairs.append((source, int(np.ravel_multi_index(goal, SIZES))))
    return lax.ppermute(value, AXES, pairs)


def swap_core(value):
    return send(value, lambda x, z, y, k: (x, z, y, 1 - k))


def along_x(value, d):
    return send(value, lambda x, z, y, k: (x + d, z, y, k))


def along_y(value, d):
    return send(value, lambda x, z, y, k: (x, z, y + d, k))


def along_z(value, d):
    return send(value, lambda x, z, y, k: (x, z + d, y, k))


def first_leg(value, d):
    return send(value, lambda x, z, y, k: (x, z, y + d, k) if k == 0 else (x, z + d, y, k))


def second_leg(value, d):
    return send(value, lambda x, z, y, k: (x, z + d, y, k) if k == 0 else (x, z, y + d, k))


def gather4(value, move, index):
    out = jnp.zeros((4,) + value.shape, value.dtype)
    out = lax.dynamic_update_index_in_dim(out, value, index, 0)
    for d in (1, 2, 3):
        out = lax.dynamic_update_index_in_dim(out, move(value, d), (index - d) % 4, 0)
    return out


def gather_back(value, move):
    return jnp.stack([value] + [move(value, d) for d in (1, 2, 3)])


def softmax_rows(scores, valid):
    masked = jnp.where(valid, scores, neg_fill)
    top = jnp.max(masked, axis=-1, keepdims=True)
    expo = jnp.exp(masked - top)
    return expo / jnp.sum(expo, axis=-1, keepdims=True)


def dot(a, b):
    return jnp.dot(a, b, preferred_element_type=f32)


def rms_scale(values, gain):
    mean_sq = jnp.mean(values * values, axis=-1, keepdims=True)
    return values * lax.rsqrt(mean_sq + eps) * gain


def fine_normed(rows, gain):
    return rms_scale(rows.astype(f32), gain).astype(bf16)


def fine_attention(position, queries, keys, values):
    span = queries.shape[0]
    queries = queries.reshape(span, FH, 128)
    keys = keys.reshape(2 * span, FH, 128)
    values = values.reshape(2 * span, FH, 128)
    scores = jnp.einsum("qhd,khd->hqk", queries, keys, preferred_element_type=f32) * 128 ** (-0.5)
    query_index = jnp.arange(span, dtype=jnp.int32)[:, None]
    key_index = jnp.arange(2 * span, dtype=jnp.int32)[None, :]
    valid = (
        (key_index > query_index)
        & (key_index <= query_index + span)
        & (key_index + position * span >= span)
    )
    weights = softmax_rows(scores, valid[None]).astype(bf16)
    mixed = jnp.einsum("hqk,khd->qhd", weights, values, preferred_element_type=f32)
    return mixed.astype(bf16).reshape(span, DF)


def fold(up, gain, weight):
    rows = []
    for row in range(2):
        blocks = [up[2 * row + k, y, :384] for y in range(4) for k in range(2)]
        rows.append(jnp.concatenate(blocks, axis=1))
    block = (jnp.concatenate(rows, axis=0).astype(f32) * gain).astype(bf16)
    return dot(block, weight).astype(bf16)


def body(
    byte_in,
    flags,
    fine_gain,
    fine_qkv,
    fine_out,
    up_weight,
    coarse_gain,
    q_weight,
    kv_weight,
    out_weight,
):
    x, z, y, core = (lax.axis_index(name) for name in AXES)
    position = z * 8 + y * 2 + core
    first_index = jnp.where(core == 0, y, z)
    second_index = jnp.where(core == 0, z, y)
    columns = 32
    stretches = CPD * columns
    half = stretches // 2
    embedded = byte_in[0]
    four = jnp.arange(4, dtype=jnp.int32)

    def following(x, z, y, k):
        c = (z * 8 + y * 2 + k + 1) % 32
        return (x, c // 8, c // 2 % 4, c % 2)

    earlier = send(embedded, following)

    def turn(x, z, y, k):
        second = 2 * (x % 2) + k
        return (z, second, y, 0) if x < 2 else (z, y, second, 1)

    turned = send(up_weight, turn)

    out_turned = send(out_weight, lambda x, z, y, k: (2 * x - z, x, y, k))
    qkv = jnp.transpose(fine_qkv, (1, 0, 2))
    normed = fine_normed(embedded, fine_gain)
    normed, flags = lax.optimization_barrier((normed, flags))

    flag_row = flags[0]
    local = jnp.cumsum(flag_row) - 1
    count = jnp.sum(flag_row)
    head_len = jnp.sum((local < 0).astype(jnp.int32))
    last_len = jnp.sum((local == count - 1).astype(jnp.int32))
    lane = jnp.arange(256, dtype=jnp.int32)[None, :]
    facts = jnp.where(lane == 0, count, jnp.where(lane == 1, head_len, last_len)).astype(bf16)
    facts = jnp.broadcast_to(facts, (16, 256))
    queries = dot(normed, qkv[0]).astype(bf16)
    turned, queries, earlier, q_weight, kv_weight = lax.optimization_barrier(
        (turned, queries, earlier, q_weight, kv_weight)
    )

    payload = jnp.concatenate([turned, facts], axis=0)
    up_row = gather4(payload, first_leg, first_index)
    kv_turned = jnp.transpose(kv_weight, (1, 2, 0)).reshape(64, 2048)
    q_other = swap_core(q_weight)
    kv_far_core = swap_core(kv_turned)
    both = jnp.concatenate([fine_normed(earlier, fine_gain), normed], axis=0)
    keys = dot(both, qkv[1]).astype(bf16)
    values = dot(both, qkv[2]).astype(bf16)
    up_row, keys, values, out_turned, q_other, kv_far_core = lax.optimization_barrier(
        (up_row, keys, values, out_turned, q_other, kv_far_core)
    )

    over_x = lax.all_gather(jnp.concatenate([out_turned, up_weight], axis=0), "x", axis=0)
    kv_both = jnp.concatenate([kv_turned, kv_far_core], axis=0).T
    qkv_weight = jnp.concatenate([q_weight, q_other, kv_both], axis=1)
    up_block = gather4(up_row, second_leg, second_index)
    mixed = fine_attention(position, queries, keys, values)
    hidden = (embedded.astype(f32) + dot(mixed, fine_out)).astype(bf16)

    slot_index = jnp.arange(SLOTS, dtype=jnp.int32)
    slot_of = jnp.where(local < 0, MAXC, local)
    slot_table = slot_of[None, :] == slot_index[:, None]
    lens = jnp.sum(slot_table.astype(jnp.int32), axis=1)
    as_sum = (slot_index == MAXC) | (slot_index == count - 1)
    inverse = jnp.where(as_sum, 1.0, 1.0 / jnp.maximum(lens, 1).astype(f32)).reshape(SLOTS, 1)
    slots = (dot(slot_table.astype(bf16), hidden) * inverse).astype(bf16)
    slots = jnp.stack([slots[:, :768], slots[:, 768:]])
    mine = lax.dynamic_index_in_dim(slots, core, 0, keepdims=False)
    other = lax.dynamic_index_in_dim(slots, 1 - core, 0, keepdims=False)
    pair = jnp.stack([mine, swap_core(other)])
    pair, up_block, qkv_weight = lax.optimization_barrier((pair, up_block, qkv_weight))
    slots_row = gather_back(pair, first_leg)

    facts = up_block[:, :, 384, :128].astype(f32)
    facts = jnp.where(core == 0, facts, jnp.swapaxes(facts, 0, 1)).reshape(16, 128)
    facts_other = swap_core(facts)
    facts = jnp.where(
        core == 0, jnp.stack([facts, facts_other], axis=1), jnp.stack([facts_other, facts], axis=1)
    )
    facts = facts.reshape(columns, 128).astype(jnp.int32)
    counts = facts[:, 0]
    begins = jnp.cumsum(counts) - counts
    whole_last = facts[:, 2] + jnp.concatenate([facts[1:, 1], jnp.zeros((1,), jnp.int32)])

    gain_block = lax.dynamic_slice_in_dim(coarse_gain, x * 2048, 2048, 0)
    folded = fold(up_block, gain_block, qkv_weight).reshape(4, 192, 640)
    folded, slots_row = lax.optimization_barrier((folded, slots_row))
    total = lax.dynamic_index_in_dim(folded, x, 0, keepdims=False).astype(f32)
    all_slots = gather_back(slots_row, second_leg)
    for d in (1, 2, 3):
        piece = lax.dynamic_index_in_dim(folded, (x + d) % 4, 0, keepdims=False)
        total = total + along_x(piece, d).astype(f32)
    total = total.astype(bf16)
    total_far = [along_x(total, d) for d in (1, 2, 3)]

    all_slots = all_slots.reshape(columns * SLOTS, 768)

    first_of = (first_index - four[None, :, None]) % 4
    second_of = (second_index - four[:, None, None]) % 4
    core_of = jnp.array([0, 1], jnp.int32)[None, None, :] ^ core
    device_of = jnp.where(core == 0, second_of * 8 + first_of * 2, first_of * 8 + second_of * 2)
    device_of = (device_of + core_of).reshape(columns, 1)
    is_device = device_of == jnp.arange(columns, dtype=jnp.int32)[None, :]
    begin_of = jnp.sum(jnp.where(is_device, begins[None, :], 0), axis=1, keepdims=True)
    count_of = jnp.sum(jnp.where(is_device, counts[None, :], 0), axis=1, keepdims=True)
    place = jnp.where(
        slot_index[None, :] == MAXC,
        begin_of - 1,
        jnp.where(slot_index[None, :] < count_of, begin_of + slot_index[None, :], -1),
    ).reshape(1, columns * SLOTS)
    choose = (place == jnp.arange(stretches, dtype=jnp.int32)[:, None]).astype(bf16)
    row = jnp.arange(stretches, dtype=jnp.int32)[:, None]
    is_last = row == (begins + counts - 1)[None, :]
    row_len = jnp.sum(jnp.where(is_last, whole_last[None, :], 0), axis=1, keepdims=True)
    row_scale = 1.0 / jnp.maximum(row_len, 1).astype(f32)
    pooled = (dot(choose, all_slots) * row_scale).astype(bf16)
    pooled_other = swap_core(pooled)
    pooled, *total_far = lax.optimization_barrier((pooled, *total_far))
    folded = lax.dynamic_update_index_in_dim(jnp.zeros((4, 192, 640), bf16), total, x, 0)
    for d, block in enumerate(total_far, 1):
        folded = lax.dynamic_update_index_in_dim(folded, block, (x - d) % 4, 0)
    folded = folded.reshape(768, 640)
    arrived = swap_core(folded[:, 256:])
    q_cols = jnp.stack([folded[:, :256], arrived[:, :256]])
    kv_mine = jnp.stack([folded[:, 512:576], arrived[:, 320:]])
    kv_other = jnp.stack([folded[:, 576:], arrived[:, 256:320]])
    kv_near = jnp.where(
        core == 0,
        jnp.concatenate([kv_mine, kv_other], axis=2),
        jnp.concatenate([kv_other, kv_mine], axis=2),
    )
    kv_far = send(kv_near, lambda x, z, y, k: (x, z, y ^ 1, k))
    pooled_other, out_mine = lax.optimization_barrier((pooled_other, over_x))
    up_cols = out_mine[:, 2048:].reshape(2, 768, 256)
    up_cols = jnp.where(core == 0, up_cols, up_cols[::-1])

    out_other = swap_core(out_mine)
    out_rows = []
    for d in range(4):
        pieces = []
        for e in range(4):
            at = ((z - e) % 4, (y - d) % 4 * 512, 0)
            own = lax.dynamic_slice(out_mine, at, (1, 512, 256))[0]
            far = lax.dynamic_slice(out_other, at, (1, 512, 256))[0]
            pieces += [own, far]
        out_rows.append(jnp.concatenate(pieces, axis=1))
    out_block = jnp.concatenate(out_rows, axis=0)


    up_out = dot(pooled, up_cols[0]) + dot(pooled_other, up_cols[1])
    coarse_in = up_out.astype(bf16)
    coarse_f32 = coarse_in.astype(f32)
    squares = jnp.sum(coarse_f32 * coarse_f32, axis=1).reshape(1, stretches)
    squares = squares + swap_core(squares)
    squares = squares + sum(along_y(squares, d) for d in (1, 2, 3))
    squares, kv_far = lax.optimization_barrier((squares, kv_far))
    kv_all = jnp.where(
        y % 2 == 0,
        jnp.concatenate([kv_near, kv_far], axis=2),
        jnp.concatenate([kv_far, kv_near], axis=2),
    )
    kv_all = kv_all.reshape(2, 768, 4, 2, 32).transpose(0, 1, 3, 2, 4).reshape(2, 768, 256)
    weights_all = jnp.concatenate([q_cols, kv_all], axis=2)
    squares = squares + sum(along_z(squares, d) for d in (1, 2, 3))
    scale = lax.rsqrt(squares / DC + eps).reshape(stretches, 1)
    qkv = dot(pooled, weights_all[0]) + dot(pooled_other, weights_all[1])
    qkv = (qkv * scale).astype(bf16)
    head = DC // HEADS
    queries = qkv[:, :256].reshape(stretches, 2, head)
    keys = qkv[:, 256 : 256 + head]
    values = qkv[:, 256 + head :]
    scores = jnp.einsum("qhd,kd->hqk", queries, keys, preferred_element_type=f32) * head ** (-0.5)
    rows = jnp.arange(stretches, dtype=jnp.int32)
    causal = rows[:, None] >= rows[None, :]
    coarse_weights = softmax_rows(scores, causal).astype(bf16)
    mix = jnp.einsum("hqk,kd->qhd", coarse_weights, values, preferred_element_type=f32)
    mix = mix.astype(bf16).reshape(2, half, 256)

    mine = lax.dynamic_index_in_dim(mix, core, 0, keepdims=False)
    other = lax.dynamic_index_in_dim(mix, 1 - core, 0, keepdims=False)
    got = swap_core(other)
    pair = jnp.where(
        core == 0, jnp.concatenate([mine, got], axis=1), jnp.concatenate([got, mine], axis=1)
    )
    branches = []
    for part in (pair[: half // 2], pair[half // 2 :]):
        group = jnp.concatenate([part] + [along_y(part, d) for d in (1, 2, 3)], axis=1)
        partial = dot(group, out_block)
        branch = partial[:, :512]
        for d in (1, 2, 3):
            piece = partial[:, d * 512 : (d + 1) * 512].astype(bf16)
            branch = branch + along_z(piece, d).astype(f32)
        branches.append(branch)
    branch = jnp.concatenate(branches, axis=0)
    branch_other = swap_core(branch[:, 256:].astype(bf16)).astype(f32)
    branch = jnp.where(
        core == 0,
        jnp.stack([branch[:, :256], branch_other]),
        jnp.stack([branch_other, branch[:, :256]]),
    ).reshape(stretches, 256)
    coarse_out = (coarse_f32 + branch).astype(bf16)
    return (hidden.reshape(1, 128, DF), coarse_out.reshape(1, stretches, 256))


def solution(mesh):
    grid = Mesh(mesh.devices.reshape(SIZES), AXES)
    col = ("z", "y", "core")
    in_specs = (
        P("x", col, None),
        P("x", col),
        P(),
        P(),
        P(),
        P("x", col),
        P(),
        P("x", col),
        P("x", None, col),
        P("x", col),
    )
    out_specs = (P("x", col, None), P("x", None, col))
    return jax.shard_map(body, mesh=grid, in_specs=in_specs, out_specs=out_specs, check_vma=False)
```
